32 devices in a mesh: groups: 2 (over y), dp: 4 (over z), tensor: 2 (over x), pair: 2 (over core).
Axes of the slice: x: 2, y: 2, z: 4, core: 2. Of those that a mesh axis runs over, the one named last changes fastest.
Arguments:
- activations: bfloat16 [8192, 4096], P(('groups', 'dp'), ('tensor', 'pair')), parts along dimension 0, may hold values from -6 to 6
- tile_dest: int32 [8, 8], P('groups'), parts along dimension 0, may hold values from -1 to 3, as said below
- segment_ids: int32 [8, 8, 128], P('groups'), parts along dimension 0, may hold values from 0 to 2, never falling along the last dimension, each value on 1 to 96 neighbouring positions
- norm_gain: bfloat16 [4096], replicated, may hold values from 0.099609375 to 1.8984375
- q_weight: bfloat16 [4096, 4096], P('dp', ('tensor', 'pair')), may hold values from -0.09375 to 0.09375
- k_weight: bfloat16 [4096, 1024], P('dp', 'tensor'), may hold values from -0.09375 to 0.09375
- v_weight: bfloat16 [4096, 1024], P('dp', 'tensor'), may hold values from -0.09375 to 0.09375
- q_bias: bfloat16 [4096], P(('tensor', 'pair')), may hold values from -100 to 100
- k_bias: bfloat16 [1024], P('tensor'), may hold values from -24 to 24
- v_bias: bfloat16 [1024], P('tensor'), may hold values from -6 to 6
- o_weight: bfloat16 [4096, 4096], P(('tensor', 'pair'), 'dp'), may hold values from -0.25 to 0.25
Outputs:
- layer_out: bfloat16 [4096, 4096], P(('groups', 'dp'), ('tensor', 'pair')), parts along dimension 0
The draws below stay inside these ranges and needn't reach their ends.
There are 2 independent parts, one for each index of `groups`. The reference program is written for one: setup_inputs(seed, part) draws one part's arguments, and reference() takes and returns one part's arrays. A program takes and returns all parts, laid end to end along the dimension named above; an argument that names none is the same for every part. Nothing has to cross between parts.
Inputs may be any that keep to these rules, and one draw needn't show every extreme that they name: `tile_dest`: for each of the 8 slots of each dp index, the dp index its tile goes to, or -1 where the slot is empty; a dp index's tiles fill its first slots; every dp index receives exactly 4 tiles; at most 2 tiles go from one dp index to any one, and some pair reaches 2; some dp index fills all 8 slots. `segment_ids`: within each tile the segment number never falls; each segment of a tile holds at most 96 rows, and some segment exactly that many.
All inputs are finite; a program needn't handle non-finite values.
Results may differ from the reference program's by a relative error of at most 0.014.
The reference program's roundings to bfloat16 on the way count: a program that leaves them out, or rounds other values in their place, can miss the bound.
Values may be sent and summed in bfloat16 or wider, within the bound.
No kernel may reach another device: no remote copies, remote signals or barrier semaphores. Data moves between devices by JAX's collectives and lax.ppermute only.
A program may use at most 128 MiB of HBM per device.

```python
import math
import jax
import jax.numpy as jnp
import numpy as np
from jax import lax

D = 4096
QHEADS = 32
KVH = 8
HEAD = 128
TILE = 128
TPD = 4
SRC_TILES = 8
TOKENS = 2048
N_DP = 4
N_TENSOR = 2
N_PAIR = 2


def draw_k_bias(key, part):
    key = jax.random.fold_in(key, 5)
    noise_part = jax.random.normal(key, (KVH * HEAD,), jnp.float32)
    return noise_part.astype(jnp.bfloat16)


def draw_q_bias(key, part):
    key = jax.random.fold_in(key, 7)
    noise_key = jax.random.fold_in(key, 0)
    noise_part = jax.random.normal(noise_key, (QHEADS * HEAD,), jnp.float32)
    return noise_part.astype(jnp.bfloat16)


def draw_tile_dest(key, part):
    key = jax.random.fold_in(key, 11)
    order_key, cut_key, spin_key = jax.random.split(key, 3)
    block_count = N_DP // 4
    busiest = SRC_TILES
    first_cut = jax.random.randint(cut_key, (block_count,), 1, busiest, dtype=jnp.int32)
    second_key = jax.random.fold_in(cut_key, 1)
    second_cut = jax.random.randint(second_key, (block_count,), 1, busiest - 1, dtype=jnp.int32)
    second_cut = second_cut + (second_cut >= first_cut).astype(jnp.int32)
    lower_cut = jnp.minimum(first_cut, second_cut)
    upper_cut = jnp.maximum(first_cut, second_cut)
    block_loads = jnp.stack([jnp.full((block_count,), busiest, jnp.int32), lower_cut, upper_cut - lower_cut, busiest - upper_cut], axis=1).reshape(-1)
    shuffle = jax.random.permutation(order_key, N_DP)
    tile_loads = jnp.zeros((N_DP,), jnp.int32).at[shuffle].set(block_loads)
    starts = jnp.cumsum(tile_loads) - tile_loads
    slot_ids = jnp.arange(SRC_TILES, dtype=jnp.int32)
    global_index = starts[:, None] + slot_ids[None, :]
    targets = jax.random.permutation(spin_key, N_DP).astype(jnp.int32)
    destination = targets[global_index % N_DP]
    return jnp.where(slot_ids[None, :] < tile_loads[:, None], destination, -1).astype(jnp.int32)


def level_of(own_key, extent, pieces, least, high):
    def one(position, shards_of):
        draws = jax.random.uniform(jax.random.fold_in(jax.random.fold_in(own_key, 6), position), (shards_of,), jnp.float32, least / len(pieces), high / len(pieces))
        return jnp.repeat(jnp.exp(draws), extent[position] // shards_of).reshape((-1,) + (1,) * (len(extent) - position - 1))

    gain = one(*pieces[0])
    for cut in pieces[1:]:
        gain = gain * one(*cut)
    return gain


def profile(number_of, total, limit, lean):
    weights = [(1 << 20) // math.isqrt(grade ** lean) + 1 for grade in range(2, number_of + 1)]
    rest, given = total - limit - (number_of - 1), [1] * (number_of - 1)
    while rest > 0:
        candidates = [i for i in range(number_of - 1) if given[i] < limit]
        pool, remaining = sum([weights[i] for i in candidates]), rest
        for i in candidates:
            extra = min(limit - given[i], max(1, remaining * weights[i] // pool), rest)
            given[i] = given[i] + extra
            rest = rest - extra
    return np.array([limit] + given)


def uneven(key, count, total, reach, lean):
    if count == 2:
        one = jax.random.randint(key, (), max(1, total - reach), min(reach, total - 1) + 1)
        return jnp.stack([one, total - one])
    lengths = jnp.asarray(profile(count, total, reach, lean), jnp.int32)
    twos = (count - 1) // 2
    source_of, taker = lengths[1:1 + 2 * twos:2], lengths[2:2 + 2 * twos:2]
    room = jnp.minimum(source_of - 1, reach - taker)
    shifted = jax.random.randint(jax.random.fold_in(key, 1), (twos,), 0, 1 << 20) % (room + 1)
    lengths = lengths.at[1:1 + 2 * twos:2].set(source_of - shifted).at[2:2 + 2 * twos:2].set(taker + shifted)
    return lengths[jax.random.permutation(jax.random.fold_in(key, 2), count)]


def gaussian(rng, shape, deviation, limit, cuts=(), kind=jnp.bfloat16):
    drawn = jax.random.normal(rng, shape, jnp.float32) * deviation
    if len(cuts) > 0:
        drawn = level_of(rng, shape, cuts, -0.22, 0.18) * drawn
    return jnp.clip(drawn, min=-limit, max=limit).astype(kind)


def setup_inputs(seed: int = 0, part: int = 0) -> dict:
    seeds = jax.random.split(jax.random.key(seed), 12)
    own_keys = jax.random.split(jax.random.fold_in(seeds[11], part), 12)
    return {
        "activations": gaussian(own_keys[0], (N_DP * SRC_TILES * TILE, D), 1.0, 6.0, ((0, 4), (1, 4))),
        "tile_dest": draw_tile_dest(jax.random.fold_in(jax.random.fold_in(seeds[11], part), 71), part),
        "segment_ids": jax.vmap(lambda own: jnp.searchsorted(jnp.cumsum(uneven(own, 3, TILE, 3 * TILE // 4, 0)), jnp.arange(TILE), side="right"))(jax.random.split(own_keys[2], N_DP * SRC_TILES)).reshape((N_DP, SRC_TILES, TILE)).astype(jnp.int32),
        "norm_gain": jnp.clip(1.0 + 0.18 * jax.random.normal(seeds[3], (D,), jnp.float32), 0.099609375, 1.8984375).astype(jnp.bfloat16),
        "q_weight": gaussian(seeds[4], (D, QHEADS * HEAD), D ** -0.5, 0.09375, ((0, 4), (1, 4))),
        "k_weight": gaussian(seeds[5], (D, KVH * HEAD), D ** -0.5, 0.09375, ((0, 4), (1, 2))),
        "v_weight": gaussian(seeds[6], (D, KVH * HEAD), D ** -0.5, 0.09375, ((0, 4), (1, 2))),
        "q_bias": draw_q_bias(jax.random.fold_in(seeds[11], 71), part),
        "k_bias": draw_k_bias(jax.random.fold_in(seeds[11], 71), part),
        "v_bias": gaussian(seeds[9], (KVH * HEAD,), 1.0, 6.0, ((0, 2),)),
        "o_weight": gaussian(seeds[10], (QHEADS * HEAD, D), (QHEADS * HEAD // 8) ** -0.5, 0.25, ((0, 4), (1, 4))),
    }


norm_eps = 1e-06

def normalize(values, gain_vector):
    widened = values.astype(jnp.float32)
    meansq = lax.optimization_barrier(jnp.mean(widened * widened, axis=-1, keepdims=True))
    return (widened * lax.rsqrt(meansq + norm_eps) * gain_vector.astype(jnp.float32)).astype(jnp.bfloat16)

def rotary(values, positions):
    half_size = values.shape[-1] // 2
    inverse = jnp.power(jnp.float32(1000000.0), -2.0 * jnp.arange(half_size, dtype=jnp.float32) / values.shape[-1])
    angles = positions.astype(jnp.float32)[:, None] * inverse[None, :]
    cosine = jnp.cos(angles)[:, None, :]
    sine_part = jnp.sin(angles)[:, None, :]
    front_half = values[..., :half_size]
    back_half = values[..., half_size:]
    return jnp.concatenate([front_half * cosine - back_half * sine_part, back_half * cosine + front_half * sine_part], axis=-1)

def tile_order(tile_dest):
    flat_plan = tile_dest.reshape(-1).astype(jnp.int32)
    slot_ids = jnp.arange(flat_plan.shape[0], dtype=jnp.int32)
    targets = jnp.arange(N_DP, dtype=jnp.int32)
    member = (flat_plan[None, :] == targets[:, None]).astype(jnp.int32)
    ranking = (jnp.cumsum(member, axis=1) - 1).astype(jnp.int32)
    wanted = jnp.arange(TPD, dtype=jnp.int32)
    picked = member[:, None, :] * (ranking[:, None, :] == wanted[None, :, None]).astype(jnp.int32)
    return lax.optimization_barrier(jnp.sum(picked * slot_ids[None, None, :], axis=2)).astype(jnp.int32)

def tile_positions(segment):
    earlier = (segment[..., None, :] < segment[..., :, None]).astype(jnp.int32)
    first_row = lax.optimization_barrier(jnp.sum(earlier, axis=-1)).astype(jnp.int32)
    return (jnp.arange(segment.shape[-1], dtype=jnp.int32) - first_row).astype(jnp.int32)

def attend_tiles(block_parts):
    query_rows, key_rows, value_rows, segment = block_parts
    query_groups = query_rows.astype(jnp.float32).reshape(TPD, TILE, KVH, QHEADS // KVH, HEAD)
    scores = jnp.einsum('tqgsd,tkgd->tgsqk', query_groups, key_rows.astype(jnp.float32)) * (1.0 / math.sqrt(HEAD))
    places = jnp.arange(TILE, dtype=jnp.int32)
    allowed = (segment[:, :, None] == segment[:, None, :]) & (places[None, None, :] <= places[None, :, None])
    scores = jnp.where(allowed[:, None, None, :, :], scores, -1e+30)
    attn_probs = jax.nn.softmax(scores, axis=-1).astype(jnp.bfloat16)
    context = jnp.einsum('tgsqk,tkgd->tqgsd', attn_probs.astype(jnp.float32), value_rows.astype(jnp.float32))
    return context.astype(jnp.bfloat16).reshape(TPD * TILE, QHEADS * HEAD)

def reference(activations, tile_dest, segment_ids, norm_gain, q_weight, k_weight, v_weight, q_bias, k_bias, v_bias, o_weight):
    order_ids = tile_order(tile_dest).reshape(-1)
    source_tiles = activations.reshape(N_DP * SRC_TILES, TILE, D)
    packed = jnp.take(source_tiles, order_ids, axis=0).reshape(TOKENS, D)
    tile_segments = jnp.take(segment_ids.reshape(N_DP * SRC_TILES, TILE).astype(jnp.int32), order_ids, axis=0)
    positions = tile_positions(tile_segments).reshape(TOKENS)
    normed = normalize(packed, norm_gain)
    q_lin = jnp.dot(normed, q_weight, preferred_element_type=jnp.float32) + q_bias.astype(jnp.float32)
    queries = rotary(q_lin.reshape(TOKENS, QHEADS, HEAD), positions).astype(jnp.bfloat16)
    k_lin = jnp.dot(normed, k_weight, preferred_element_type=jnp.float32) + k_bias.astype(jnp.float32)
    keys_all = rotary(k_lin.reshape(TOKENS, KVH, HEAD), positions).astype(jnp.bfloat16)
    v_lin = jnp.dot(normed, v_weight, preferred_element_type=jnp.float32) + v_bias.astype(jnp.float32)
    values_all = v_lin.astype(jnp.bfloat16).reshape(TOKENS, KVH, HEAD)
    blocks = (queries.reshape(N_DP, TPD, TILE, QHEADS, HEAD), keys_all.reshape(N_DP, TPD, TILE, KVH, HEAD), values_all.reshape(N_DP, TPD, TILE, KVH, HEAD), tile_segments.reshape(N_DP, TPD, TILE))
    context = lax.map(attend_tiles, blocks).reshape(TOKENS, QHEADS * HEAD)
    share_count = N_TENSOR * N_PAIR
    share_width = QHEADS * HEAD // share_count

    def add_share(share_index, running):
        columns_part = lax.dynamic_slice_in_dim(context, share_index * share_width, share_width, 1)
        weight_rows = lax.dynamic_slice_in_dim(o_weight, share_index * share_width, share_width, 0)
        part_sum = jnp.dot(columns_part, weight_rows, preferred_element_type=jnp.float32).astype(jnp.bfloat16)
        part_sum = lax.optimization_barrier(part_sum)
        return running + part_sum.astype(jnp.float32)
    summed = lax.fori_loop(0, share_count, add_share, jnp.zeros((TOKENS, D), jnp.float32))
    return (packed.astype(jnp.float32) + summed).astype(jnp.bfloat16)
```

```python
import math

import jax
import jax.numpy as jnp
from jax import lax
from jax.experimental import pallas as pl
from jax.experimental.pallas import tpu as pltpu
from jax.sharding import PartitionSpec as P

QHEADS = 32
KVH = 8
HEAD = 128
TPD = 4
GROUP_SIZE = QHEADS // KVH


norm_eps = 1e-06

def normalize(values, gain_vector):
    widened = values.astype(jnp.float32)
    meansq = jnp.mean(widened * widened, axis=-1, keepdims=True)
    return (widened * lax.rsqrt(meansq + norm_eps) * gain_vector.astype(jnp.float32)).astype(
        jnp.bfloat16
    )


def rotary(values, positions):
    half_size = values.shape[-1] // 2
    inverse = jnp.power(
        jnp.float32(1000000.0), -2.0 * jnp.arange(half_size, dtype=jnp.float32) / values.shape[-1]
    )
    angles = positions.astype(jnp.float32)[:, None] * inverse[None, :]
    cosine = jnp.cos(angles)[:, None, :]
    sine_part = jnp.sin(angles)[:, None, :]
    front_half = values[..., :half_size]
    back_half = values[..., half_size:]
    return jnp.concatenate(
        [front_half * cosine - back_half * sine_part, back_half * cosine + front_half * sine_part],
        axis=-1,
    )


def tile_positions(segment):
    earlier = (segment[..., None, :] < segment[..., :, None]).astype(jnp.int32)
    first_row = jnp.sum(earlier, axis=-1)
    return jnp.arange(segment.shape[-1], dtype=jnp.int32) - first_row


def attend_tiles(query_groups, key_rows, value_rows, segment):
    tile_rows = query_groups.shape[1]
    scores = jnp.einsum(
        "tqgsd,tkgd->tgsqk", query_groups, key_rows, preferred_element_type=jnp.float32
    )
    scores = scores * (1.0 / math.sqrt(query_groups.shape[-1]))
    places = jnp.arange(tile_rows, dtype=jnp.int32)
    allowed = (segment[:, :, None] == segment[:, None, :]) & (
        places[None, None, :] <= places[None, :, None]
    )
    scores = jnp.where(allowed[:, None, None, :, :], scores, -1e30)
    attn_probs = jax.nn.softmax(scores, axis=-1).astype(jnp.bfloat16)
    context = jnp.einsum(
        "tgsqk,tkgd->tqgsd", attn_probs, value_rows, preferred_element_type=jnp.float32
    )
    return context.astype(jnp.bfloat16)


def body(
    activations,
    tile_dest,
    segment_ids,
    norm_gain,
    q_weight,
    k_weight,
    v_weight,
    q_bias,
    k_bias,
    v_bias,
    o_weight,
):
    dp_count = lax.axis_size("dp")
    own_index = lax.axis_index("dp")
    pair_size = lax.axis_size("pair")
    pair_index = lax.axis_index("pair")
    slot_count = tile_dest.shape[1]
    tile_rows = segment_ids.shape[2]
    feature_share = activations.shape[1]
    peer_slots = (slot_count + dp_count - 1) // dp_count
    own_plan = lax.dynamic_index_in_dim(tile_dest, own_index, 0, keepdims=False)
    slot_ids = jnp.arange(slot_count, dtype=jnp.int32)
    targets = jnp.arange(dp_count, dtype=jnp.int32)
    peer_ids = jnp.arange(peer_slots, dtype=jnp.int32)
    earlier_same = (own_plan[None, :] == own_plan[:, None]) & (
        slot_ids[None, :] < slot_ids[:, None]
    )
    send_rank = jnp.sum(earlier_same.astype(jnp.int32), axis=1)
    chooser = (own_plan[None, None, :] == targets[:, None, None]) & (
        send_rank[None, None, :] == peer_ids[None, :, None]
    )
    own_tiles = activations.reshape(slot_count, tile_rows, feature_share)
    outgoing = jnp.einsum(
        "jps,srf->jprf", chooser.astype(jnp.bfloat16), own_tiles, preferred_element_type=jnp.float32
    ).astype(jnp.bfloat16)
    arrived = lax.all_to_all(outgoing, "dp", split_axis=0, concat_axis=0, tiled=True)
    to_here = (tile_dest == own_index).astype(jnp.int32)
    from_each = jnp.sum(to_here, axis=1)
    first_place = jnp.cumsum(from_each) - from_each
    place_of = first_place[:, None] + peer_ids[None, :]
    landed = peer_ids[None, :] < from_each[:, None]
    tile_ids = jnp.arange(TPD, dtype=jnp.int32)
    placer = (place_of[None, :, :] == tile_ids[:, None, None]) & landed[None, :, :]
    packed_tiles = jnp.einsum(
        "ksp,sprf->krf", placer.astype(jnp.bfloat16), arrived, preferred_element_type=jnp.float32
    ).astype(jnp.bfloat16)
    row_count = TPD * tile_rows
    packed = packed_tiles.reshape(row_count, feature_share)
    flat_plan = tile_dest.reshape(-1)
    flat_member = (flat_plan == own_index).astype(jnp.int32)
    flat_rank = jnp.cumsum(flat_member) - 1
    picker = flat_member[None, :] * (flat_rank[None, :] == tile_ids[:, None]).astype(jnp.int32)
    flat_segments = segment_ids.reshape(-1, tile_rows)
    segment = jnp.sum(picker[:, :, None] * flat_segments[None, :, :], axis=1)
    positions = tile_positions(segment).reshape(row_count)
    whole_rows = lax.all_gather(packed, ("tensor", "pair"), axis=1, tiled=True)
    normed = normalize(whole_rows, norm_gain)
    q_width = q_weight.shape[1]
    kv_width = k_weight.shape[1]
    q_lin = jnp.dot(
        normed,
        lax.all_gather(q_weight, "dp", axis=0, tiled=True),
        preferred_element_type=jnp.float32,
    )
    k_lin = jnp.dot(
        normed,
        lax.all_gather(k_weight, "dp", axis=0, tiled=True),
        preferred_element_type=jnp.float32,
    )
    v_lin = jnp.dot(
        normed,
        lax.all_gather(v_weight, "dp", axis=0, tiled=True),
        preferred_element_type=jnp.float32,
    )
    q_heads = q_width // HEAD
    kv_heads = kv_width // HEAD
    queries = rotary(
        (q_lin + q_bias.astype(jnp.float32)).reshape(row_count, q_heads, HEAD), positions
    ).astype(jnp.bfloat16)
    keys_local = rotary(
        (k_lin + k_bias.astype(jnp.float32)).reshape(-1, kv_heads, HEAD), positions
    ).astype(jnp.bfloat16)
    values_local = (
        (v_lin + v_bias.astype(jnp.float32)).astype(jnp.bfloat16).reshape(-1, kv_heads, HEAD)
    )
    key_rows, value_rows = (keys_local, values_local)
    group_size = QHEADS // KVH
    kv_count = max(1, q_heads // group_size)
    group_span = q_heads // kv_count
    kv_first = pair_index * q_heads // group_size
    key_rows = lax.dynamic_slice_in_dim(key_rows, kv_first, kv_count, 1).reshape(
        TPD, tile_rows, kv_count, HEAD
    )
    value_rows = lax.dynamic_slice_in_dim(value_rows, kv_first, kv_count, 1).reshape(
        TPD, tile_rows, kv_count, HEAD
    )
    query_groups = queries.reshape(TPD, tile_rows, kv_count, group_span, HEAD)
    context = attend_tiles(query_groups, key_rows, value_rows, segment).reshape(
        row_count, q_heads * HEAD
    )
    partials = jnp.dot(
        context,
        lax.all_gather(o_weight, "dp", axis=1, tiled=True),
        preferred_element_type=jnp.float32,
    )
    full_sums = lax.psum(partials.astype(jnp.bfloat16), ("tensor", "pair")).astype(jnp.float32)
    my_slot = lax.axis_index("tensor") * pair_size + pair_index
    summed = lax.dynamic_slice_in_dim(full_sums, my_slot * feature_share, feature_share, 1)
    return (packed.astype(jnp.float32) + summed).astype(jnp.bfloat16)


def shift(values, axis, pairs):
    return lax.ppermute(values, axis, pairs)


SWAP = [(0, 1), (1, 0)]


def attention_kernel(lin_ref, bias_ref, cos_ref, sin_ref, pos_ref, out_ref):
    heads = out_ref.shape[1] // HEAD
    rows = lin_ref.shape[0]
    lin = lin_ref[...] + bias_ref[...]
    cosine = cos_ref[...]
    sine = sin_ref[...]

    def rotate(values):
        return (values * cosine + pltpu.roll(values, HEAD // 2, 1) * sine).astype(jnp.bfloat16)

    queries = jnp.concatenate(
        [rotate(lin[:, h * HEAD : (h + 1) * HEAD]) for h in range(heads)], axis=0
    )
    keys = rotate(lin[:, heads * HEAD : (heads + 1) * HEAD])
    value_rows = lin[:, (heads + 1) * HEAD :].astype(jnp.bfloat16)
    scores = lax.dot_general(
        queries, keys, (((1,), (1,)), ((), ())), preferred_element_type=jnp.float32
    )
    scores = (scores * (1.0 / math.sqrt(HEAD))).reshape(heads, rows, rows)
    row = lax.broadcasted_iota(jnp.int32, (rows, rows), 0)
    column = lax.broadcasted_iota(jnp.int32, (rows, rows), 1)
    allowed = (column <= row) & (column >= row - pos_ref[...])
    scores = jnp.where(allowed[None], scores, -1e30)
    largest = jnp.max(scores, axis=-1, keepdims=True)
    weights = jnp.exp(scores - largest)
    probs = (weights / jnp.sum(weights, axis=-1, keepdims=True)).astype(jnp.bfloat16)
    context = lax.dot_general(
        probs.reshape(heads * rows, rows),
        value_rows,
        (((1,), (0,)), ((), ())),
        preferred_element_type=jnp.float32,
    ).astype(jnp.bfloat16)
    for h in range(heads):
        out_ref[:, h * HEAD : (h + 1) * HEAD] = context[h * rows : (h + 1) * rows]


def attend_rows(lin, bias, cosine, sine, positions, tile_rows):
    count, width = lin.shape
    out_width = width - 2 * HEAD
    by_tile = lambda w: pl.BlockSpec((tile_rows, w), lambda i: (i, 0))
    return pl.pallas_call(
        attention_kernel,
        grid=(count // tile_rows,),
        in_specs=[
            by_tile(width),
            pl.BlockSpec((1, width), lambda i: (0, 0)),
            by_tile(HEAD),
            by_tile(HEAD),
            by_tile(1),
        ],
        out_specs=by_tile(out_width),
        out_shape=jax.ShapeDtypeStruct((count, out_width), jnp.bfloat16),
        compiler_params=pltpu.CompilerParams(vmem_limit_bytes=32 * 1024 * 1024),
        cost_estimate=pl.CostEstimate(
            flops=4 * count * tile_rows * out_width,
            bytes_accessed=count * (4 * width + 2 * out_width),
            transcendentals=count * out_width,
        ),
    )(lin, bias, cosine, sine, positions)


def ring_body(
    activations,
    tile_dest,
    segment_ids,
    norm_gain,
    q_weight,
    k_weight,
    v_weight,
    q_bias,
    k_bias,
    v_bias,
    o_weight,
):
    z = lax.axis_index("dp")
    y = lax.axis_index("groups")
    x = lax.axis_index("tensor")
    core = lax.axis_index("pair")
    t = x * 2 + core
    slots, tile_rows = tile_dest.shape[1], segment_ids.shape[2]
    width = activations.shape[1]
    rows = TPD * tile_rows
    peers = 2
    q_share = q_weight.shape[1] // 2

    kv_at = (core * 2 + y) * HEAD
    q_own = lax.dynamic_slice_in_dim(q_weight, y * q_share, q_share, 1)
    k_own = lax.dynamic_slice_in_dim(k_weight, kv_at, HEAD, 1)
    v_own = lax.dynamic_slice_in_dim(v_weight, kv_at, HEAD, 1)
    qkv_own = jnp.concatenate([q_own, k_own, v_own], axis=1)
    o_own = lax.dynamic_slice_in_dim(o_weight, y * q_share, q_share, 0)
    bias = jnp.concatenate(
        [
            lax.dynamic_slice_in_dim(q_bias, y * q_share, q_share, 0),
            lax.dynamic_slice_in_dim(k_bias, kv_at, HEAD, 0),
            lax.dynamic_slice_in_dim(v_bias, kv_at, HEAD, 0),
        ]
    ).astype(jnp.float32)[None, :]

    own_plan = lax.dynamic_index_in_dim(tile_dest, z, 0, keepdims=False)
    slot_ids = jnp.arange(slots, dtype=jnp.int32)
    peer_ids = jnp.arange(peers, dtype=jnp.int32)
    partners = jnp.arange(4, dtype=jnp.int32) ^ z
    same_before = (own_plan[None, :] == own_plan[:, None]) & (slot_ids[None, :] < slot_ids[:, None])
    send_rank = jnp.sum(same_before.astype(jnp.int32), axis=1)
    chooser = (own_plan[None, None, :] == partners[:, None, None]) & (
        send_rank[None, None, :] == peer_ids[None, :, None]
    )
    own_tiles = activations.reshape(slots, tile_rows, width)
    outgoing = [
        jnp.einsum(
            "ps,srf->prf",
            chooser[m].astype(jnp.bfloat16),
            own_tiles,
            preferred_element_type=jnp.float32,
        ).astype(jnp.bfloat16)
        for m in range(4)
    ]
    arrived = [outgoing[0]] + [
        shift(outgoing[m], "dp", [(i, i ^ m) for i in range(4)]) for m in range(1, 4)
    ]
    to_here = (tile_dest == z).astype(jnp.int32)
    from_each = jnp.sum(to_here, axis=1)
    first_place = jnp.cumsum(from_each) - from_each
    place_of = first_place[:, None] + peer_ids[None, :]
    landed = peer_ids[None, :] < from_each[:, None]
    tile_ids = jnp.arange(TPD, dtype=jnp.int32)
    placer = (place_of[None, :, :] == tile_ids[:, None, None]) & landed[None, :, :]
    placer = jnp.take(placer, partners, axis=1).astype(jnp.bfloat16)
    packed = sum(
        jnp.einsum(
            "kp,prf->krf", placer[:, m], arrived[m], preferred_element_type=jnp.float32
        )
        for m in range(4)
    ).astype(jnp.bfloat16).reshape(rows, width)

    flat_member = (tile_dest.reshape(-1) == z).astype(jnp.int32)
    flat_rank = jnp.cumsum(flat_member) - 1
    picker = flat_member[None, :] * (flat_rank[None, :] == tile_ids[:, None]).astype(jnp.int32)
    segment = jnp.sum(picker[:, :, None] * segment_ids.reshape(-1, tile_rows)[None, :, :], axis=1)
    positions = tile_positions(segment).reshape(rows, 1)
    positions = jnp.concatenate([positions, shift(positions, "groups", SWAP)], axis=0)
    half = HEAD // 2
    inverse = jnp.power(
        jnp.float32(1000000.0), -2.0 * jnp.arange(half, dtype=jnp.float32) / HEAD
    )
    angles = positions.astype(jnp.float32) * inverse[None, :]
    cosine, sine = jnp.cos(angles), jnp.sin(angles)
    cosine = jnp.concatenate([cosine, cosine], axis=1)
    sine = jnp.concatenate([-sine, sine], axis=1)

    widened = packed.astype(jnp.float32)
    squares = jnp.sum(widened * widened, axis=-1, keepdims=True)
    squares = squares + shift(squares, "pair", SWAP)
    squares = squares + shift(squares, "tensor", SWAP)
    gain = lax.dynamic_slice_in_dim(norm_gain, t * width, width, 0).astype(jnp.float32)
    normed = (widened * lax.rsqrt(squares / (4 * width) + norm_eps) * gain).astype(jnp.bfloat16)
    here = [normed, shift(normed, "groups", SWAP)]
    across = [shift(part, "tensor", SWAP) for part in here]
    here_other = [shift(part, "pair", SWAP) for part in here]
    across_other = [shift(part, "pair", SWAP) for part in across]
    shares = jnp.stack(
        [jnp.concatenate(part, axis=0) for part in (here, here_other, across, across_other)]
    )

    def ring(block):
        up, down = [block], [block]
        for s in range(1, 4):
            up.append(shift(up[-1], "dp", [(i, i + 1) for i in range(s - 1, 3)]))
            down.append(shift(down[-1], "dp", [(i + 1, i) for i in range(0, 4 - s)]))
        first = jnp.where(z % 2 == 0, down[1], up[1])
        second = up[2] + down[2]
        third = jnp.where(z == 1, down[1], jnp.where(z == 2, up[1], up[3] + down[3]))
        return [block, first, second, third]

    qkv_blocks = ring(qkv_own)
    o_blocks = ring(o_own)
    lin = None
    for m in range(4):
        share = lax.dynamic_index_in_dim(shares, (z ^ m) ^ t, 0, keepdims=False)
        part = jnp.dot(share, qkv_blocks[m], preferred_element_type=jnp.float32)
        lin = part if lin is None else lin + part
    context = attend_rows(lin, bias, cosine, sine, positions, tile_rows)

    total = packed.astype(jnp.float32)
    every = ("groups", "dp", "tensor", "pair")
    index = lambda zz, yy, xx, cc: ((yy * 4 + zz) * 2 + xx) * 2 + cc
    for m in range(4):
        part = jnp.dot(context, o_blocks[m], preferred_element_type=jnp.float32)
        sides = [(i, j) for i in range(2) for j in range(2)]
        to_core, to_group, to_chip = [], [], []
        for zz in range(4):
            xd, cd = (zz ^ m) // 2, (zz ^ m) % 2
            to_core += [(index(zz, i, j, 1 - cd), index(zz, i, j, cd)) for i, j in sides]
            to_group += [(index(zz, i, j, cd), index(zz, 1 - i, j, cd)) for i, j in sides]
            to_chip += [(index(zz, i, 1 - xd, cd), index(zz, i, xd, cd)) for i in range(2)]
        part = part + shift(part.astype(jnp.bfloat16), every, to_core).astype(jnp.float32)
        mine = part[:rows] + shift(part[rows:].astype(jnp.bfloat16), every, to_group).astype(
            jnp.float32
        )
        mine = mine + shift(mine.astype(jnp.bfloat16), every, to_chip).astype(jnp.float32)
        total = total + jnp.where(z ^ m == t, mine, 0.0)
    return total.astype(jnp.bfloat16)


def solution(mesh):
    shape = dict(mesh.shape)
    ringed = shape == {"groups": 2, "dp": 4, "tensor": 2, "pair": 2}
    return jax.shard_map(
        ring_body if ringed else body,
        mesh=mesh,
        in_specs=(
            P(("groups", "dp"), ("tensor", "pair")),
            P("groups", None),
            P("groups", None, None),
            P(),
            P("dp", ("tensor", "pair")),
            P("dp", "tensor"),
            P("dp", "tensor"),
            P(("tensor", "pair")),
            P("tensor"),
            P("tensor"),
            P(("tensor", "pair"), "dp"),
        ),
        out_specs=P(("groups", "dp"), ("tensor", "pair")),
        check_vma=False,
    )
```

```python
import math

import jax
import jax.numpy as jnp
from jax import lax
from jax.experimental import pallas as pl
from jax.experimental.pallas import tpu as pltpu
from jax.sharding import PartitionSpec as P

QHEADS = 32
KVH = 8
HEAD = 128
TPD = 4
GROUP_SIZE = QHEADS // KVH


norm_eps = 1e-06

def normalize(values, gain_vector):
    widened = values.astype(jnp.float32)
    meansq = jnp.mean(widened * widened, axis=-1, keepdims=True)
    return (widened * lax.rsqrt(meansq + norm_eps) * gain_vector.astype(jnp.float32)).astype(
        jnp.bfloat16
    )


def rotary(values, positions):
    half_size = values.shape[-1] // 2
    inverse = jnp.power(
        jnp.float32(1000000.0), -2.0 * jnp.arange(half_size, dtype=jnp.float32) / values.shape[-1]
    )
    angles = positions.astype(jnp.float32)[:, None] * inverse[None, :]
    cosine = jnp.cos(angles)[:, None, :]
    sine_part = jnp.sin(angles)[:, None, :]
    front_half = values[..., :half_size]
    back_half = values[..., half_size:]
    return jnp.concatenate(
        [front_half * cosine - back_half * sine_part, back_half * cosine + front_half * sine_part],
        axis=-1,
    )


def tile_positions(segment):
    earlier = (segment[..., None, :] < segment[..., :, None]).astype(jnp.int32)
    first_row = jnp.sum(earlier, axis=-1)
    return jnp.arange(segment.shape[-1], dtype=jnp.int32) - first_row


def attend_tiles(query_groups, key_rows, value_rows, segment):
    tile_rows = query_groups.shape[1]
    scores = jnp.einsum(
        "tqgsd,tkgd->tgsqk", query_groups, key_rows, preferred_element_type=jnp.float32
    )
    scores = scores * (1.0 / math.sqrt(query_groups.shape[-1]))
    places = jnp.arange(tile_rows, dtype=jnp.int32)
    allowed = (segment[:, :, None] == segment[:, None, :]) & (
        places[None, None, :] <= places[None, :, None]
    )
    scores = jnp.where(allowed[:, None, None, :, :], scores, -1e30)
    attn_probs = jax.nn.softmax(scores, axis=-1).astype(jnp.bfloat16)
    context = jnp.einsum(
        "tgsqk,tkgd->tqgsd", attn_probs, value_rows, preferred_element_type=jnp.float32
    )
    return context.astype(jnp.bfloat16)


def body(
    activations,
    tile_dest,
    segment_ids,
    norm_gain,
    q_weight,
    k_weight,
    v_weight,
    q_bias,
    k_bias,
    v_bias,
    o_weight,
):
    dp_count = lax.axis_size("dp")
    own_index = lax.axis_index("dp")
    pair_size = lax.axis_size("pair")
    pair_index = lax.axis_index("pair")
    slot_count = tile_dest.shape[1]
    tile_rows = segment_ids.shape[2]
    feature_share = activations.shape[1]
    peer_slots = (slot_count + dp_count - 1) // dp_count
    own_plan = lax.dynamic_index_in_dim(tile_dest, own_index, 0, keepdims=False)
    slot_ids = jnp.arange(slot_count, dtype=jnp.int32)
    targets = jnp.arange(dp_count, dtype=jnp.int32)
    peer_ids = jnp.arange(peer_slots, dtype=jnp.int32)
    earlier_same = (own_plan[None, :] == own_plan[:, None]) & (
        slot_ids[None, :] < slot_ids[:, None]
    )
    send_rank = jnp.sum(earlier_same.astype(jnp.int32), axis=1)
    chooser = (own_plan[None, None, :] == targets[:, None, None]) & (
        send_rank[None, None, :] == peer_ids[None, :, None]
    )
    own_tiles = activations.reshape(slot_count, tile_rows, feature_share)
    outgoing = jnp.einsum(
        "jps,srf->jprf", chooser.astype(jnp.bfloat16), own_tiles, preferred_element_type=jnp.float32
    ).astype(jnp.bfloat16)
    arrived = lax.all_to_all(outgoing, "dp", split_axis=0, concat_axis=0, tiled=True)
    to_here = (tile_dest == own_index).astype(jnp.int32)
    from_each = jnp.sum(to_here, axis=1)
    first_place = jnp.cumsum(from_each) - from_each
    place_of = first_place[:, None] + peer_ids[None, :]
    landed = peer_ids[None, :] < from_each[:, None]
    tile_ids = jnp.arange(TPD, dtype=jnp.int32)
    placer = (place_of[None, :, :] == tile_ids[:, None, None]) & landed[None, :, :]
    packed_tiles = jnp.einsum(
        "ksp,sprf->krf", placer.astype(jnp.bfloat16), arrived, preferred_element_type=jnp.float32
    ).astype(jnp.bfloat16)
    row_count = TPD * tile_rows
    packed = packed_tiles.reshape(row_count, feature_share)
    flat_plan = tile_dest.reshape(-1)
    flat_member = (flat_plan == own_index).astype(jnp.int32)
    flat_rank = jnp.cumsum(flat_member) - 1
    picker = flat_member[None, :] * (flat_rank[None, :] == tile_ids[:, None]).astype(jnp.int32)
    flat_segments = segment_ids.reshape(-1, tile_rows)
    segment = jnp.sum(picker[:, :, None] * flat_segments[None, :, :], axis=1)
    positions = tile_positions(segment).reshape(row_count)
    whole_rows = lax.all_gather(packed, ("tensor", "pair"), axis=1, tiled=True)
    normed = normalize(whole_rows, norm_gain)
    q_width = q_weight.shape[1]
    kv_width = k_weight.shape[1]
    q_lin = jnp.dot(
        normed,
        lax.all_gather(q_weight, "dp", axis=0, tiled=True),
        preferred_element_type=jnp.float32,
    )
    k_lin = jnp.dot(
        normed,
        lax.all_gather(k_weight, "dp", axis=0, tiled=True),
        preferred_element_type=jnp.float32,
    )
    v_lin = jnp.dot(
        normed,
        lax.all_gather(v_weight, "dp", axis=0, tiled=True),
        preferred_element_type=jnp.float32,
    )
    q_heads = q_width // HEAD
    kv_heads = kv_width // HEAD
    queries = rotary(
        (q_lin + q_bias.astype(jnp.float32)).reshape(row_count, q_heads, HEAD), positions
    ).astype(jnp.bfloat16)
    keys_local = rotary(
        (k_lin + k_bias.astype(jnp.float32)).reshape(-1, kv_heads, HEAD), positions
    ).astype(jnp.bfloat16)
    values_local = (
        (v_lin + v_bias.astype(jnp.float32)).astype(jnp.bfloat16).reshape(-1, kv_heads, HEAD)
    )
    key_rows, value_rows = (keys_local, values_local)
    group_size = QHEADS // KVH
    kv_count = max(1, q_heads // group_size)
    group_span = q_heads // kv_count
    kv_first = pair_index * q_heads // group_size
    key_rows = lax.dynamic_slice_in_dim(key_rows, kv_first, kv_count, 1).reshape(
        TPD, tile_rows, kv_count, HEAD
    )
    value_rows = lax.dynamic_slice_in_dim(value_rows, kv_first, kv_count, 1).reshape(
        TPD, tile_rows, kv_count, HEAD
    )
    query_groups = queries.reshape(TPD, tile_rows, kv_count, group_span, HEAD)
    context = attend_tiles(query_groups, key_rows, value_rows, segment).reshape(
        row_count, q_heads * HEAD
    )
    partials = jnp.dot(
        context,
        lax.all_gather(o_weight, "dp", axis=1, tiled=True),
        preferred_element_type=jnp.float32,
    )
    full_sums = lax.psum(partials.astype(jnp.bfloat16), ("tensor", "pair")).astype(jnp.float32)
    my_slot = lax.axis_index("tensor") * pair_size + pair_index
    summed = lax.dynamic_slice_in_dim(full_sums, my_slot * feature_share, feature_share, 1)
    return (packed.astype(jnp.float32) + summed).astype(jnp.bfloat16)


def shift(values, axis, pairs):
    return lax.ppermute(values, axis, pairs)


SWAP = [(0, 1), (1, 0)]


def fetch_share(which, shares, target, sem):
    def each(act):
        for k, share in enumerate(shares):

            @pl.when(which == k)
            def _():
                act(pltpu.make_async_copy(share, target, sem))

    return each


def linear_kernel(at_ref, *refs):
    shares, blocks = refs[:4], refs[4:7]
    out_ref, share_buf, block_buf, sems = refs[7:]
    fetches = []
    for m in range(3):
        fetches.append(fetch_share(at_ref[m], shares, share_buf.at[m], sems.at[m]))
        fetches[m](lambda copy: copy.start())
        pltpu.make_async_copy(blocks[m], block_buf.at[m], sems.at[3 + m]).start()
    for m in range(3):
        fetches[m](lambda copy: copy.wait())
        pltpu.make_async_copy(blocks[m], block_buf.at[m], sems.at[3 + m]).wait()
    step = 128

    @pl.loop(0, out_ref.shape[0] // step)
    def _(i):
        at = pl.ds(pl.multiple_of(i * step, step), step)
        total = None
        for m in range(3):
            part = jnp.dot(share_buf[m, at], block_buf[m], preferred_element_type=jnp.float32)
            total = part if total is None else total + part
        out_ref[at] = total


def linear_rows(at, shares, blocks):
    (count, depth), width = shares[0].shape, blocks[0].shape[1]
    return pl.pallas_call(
        linear_kernel,
        in_specs=[pl.BlockSpec(memory_space=pltpu.SMEM)]
        + [pl.BlockSpec(memory_space=pl.ANY)] * 7,
        out_specs=pl.BlockSpec(memory_space=pltpu.VMEM),
        out_shape=jax.ShapeDtypeStruct((count, width), jnp.float32),
        scratch_shapes=[
            pltpu.VMEM((3, count, depth), jnp.bfloat16),
            pltpu.VMEM((3, depth, width), jnp.bfloat16),
            pltpu.SemaphoreType.DMA((6,)),
        ],
        compiler_params=pltpu.CompilerParams(vmem_limit_bytes=32 * 1024 * 1024),
    )(at, *shares, *blocks)


def attention_kernel(at_ref, *refs):
    shares, refs = refs[:4], refs[4:]
    block_ref, lin_ref, bias_ref, cos_ref, sin_ref, pos_ref, out_ref, share_buf, sem = refs
    step = pl.program_id(0)

    @pl.when(step == 0)
    def _():
        fetch = fetch_share(at_ref[0], shares, share_buf, sem)
        fetch(lambda copy: copy.start())
        fetch(lambda copy: copy.wait())

    own = pl.ds(pl.multiple_of(step * lin_ref.shape[0], lin_ref.shape[0]), lin_ref.shape[0])

    heads = out_ref.shape[1] // HEAD
    rows = lin_ref.shape[0]
    lin = lin_ref[...] + jnp.dot(
        share_buf[own], block_ref[...], preferred_element_type=jnp.float32
    )
    lin = lin + bias_ref[...]
    cosine = cos_ref[...]
    sine = sin_ref[...]

    def rotate(values):
        return (values * cosine + pltpu.roll(values, HEAD // 2, 1) * sine).astype(jnp.bfloat16)

    queries = jnp.concatenate(
        [rotate(lin[:, h * HEAD : (h + 1) * HEAD]) for h in range(heads)], axis=0
    )
    keys = rotate(lin[:, heads * HEAD : (heads + 1) * HEAD])
    value_rows = lin[:, (heads + 1) * HEAD :].astype(jnp.bfloat16)
    scores = lax.dot_general(
        queries, keys, (((1,), (1,)), ((), ())), preferred_element_type=jnp.float32
    )
    scores = (scores * (1.0 / math.sqrt(HEAD))).reshape(heads, rows, rows)
    row = lax.broadcasted_iota(jnp.int32, (rows, rows), 0)
    column = lax.broadcasted_iota(jnp.int32, (rows, rows), 1)
    allowed = (column <= row) & (column >= row - pos_ref[...])
    scores = jnp.where(allowed[None], scores, -1e30)
    largest = jnp.max(scores, axis=-1, keepdims=True)
    weights = jnp.exp(scores - largest)
    probs = (weights / jnp.sum(weights, axis=-1, keepdims=True)).astype(jnp.bfloat16)
    context = lax.dot_general(
        probs.reshape(heads * rows, rows),
        value_rows,
        (((1,), (0,)), ((), ())),
        preferred_element_type=jnp.float32,
    ).astype(jnp.bfloat16)
    for h in range(heads):
        out_ref[:, h * HEAD : (h + 1) * HEAD] = context[h * rows : (h + 1) * rows]


def attend_rows(shares, at, block, lin, bias, cosine, sine, positions, tile_rows):
    count, width = lin.shape
    out_width = width - 2 * HEAD
    by_tile = lambda w: pl.BlockSpec((tile_rows, w), lambda i, at: (i, 0))
    return pl.pallas_call(
        attention_kernel,
        grid_spec=pltpu.PrefetchScalarGridSpec(
            num_scalar_prefetch=1,
            grid=(count // tile_rows,),
            in_specs=[
                *[pl.BlockSpec(memory_space=pl.ANY)] * 4,
                pl.BlockSpec(block.shape, lambda i, at: (0, 0)),
                by_tile(width),
                pl.BlockSpec((1, width), lambda i, at: (0, 0)),
                by_tile(HEAD),
                by_tile(HEAD),
                by_tile(1),
            ],
            out_specs=by_tile(out_width),
            scratch_shapes=[
                pltpu.VMEM(shares[0].shape, jnp.bfloat16),
                pltpu.SemaphoreType.DMA(()),
            ],
        ),
        out_shape=jax.ShapeDtypeStruct((count, out_width), jnp.bfloat16),
        compiler_params=pltpu.CompilerParams(vmem_limit_bytes=32 * 1024 * 1024),
    )(at.reshape(1), *shares, block, lin, bias, cosine, sine, positions)


def pack_kernel(slots_ref, *refs):
    for m in range(4):
        refs[4 + m][...] = refs[m][...]


def pack_tiles(send_slots, activations, tile_rows):
    width = activations.shape[1]
    tiles = activations.reshape(-1, tile_rows, width)
    peers = send_slots.shape[0] // 4
    block = (1, tile_rows, width)
    pick = lambda m: pl.BlockSpec(block, lambda p, slots: (slots[m * peers + p], 0, 0))
    outs = pl.pallas_call(
        pack_kernel,
        grid_spec=pltpu.PrefetchScalarGridSpec(
            num_scalar_prefetch=1,
            grid=(peers,),
            in_specs=[pick(m) for m in range(4)],
            out_specs=[pl.BlockSpec(block, lambda p, slots: (p, 0, 0))] * 4,
        ),
        out_shape=[jax.ShapeDtypeStruct((peers, tile_rows, width), activations.dtype)] * 4,
        cost_estimate=pl.CostEstimate(
            flops=0, bytes_accessed=4 * activations.size, transcendentals=0
        ),
    )(jnp.clip(send_slots, 0, tiles.shape[0] - 1), *[tiles] * 4)
    return [out.reshape(peers * tile_rows, width) for out in outs]


def place_kernel(picks_ref, *refs):
    arrived, (packed_ref, squares_ref, sems) = refs[:4], refs[4:]
    count = packed_ref.shape[0]

    def each(act):
        for k in range(count):
            for m in range(4):

                @pl.when(picks_ref[k] == m)
                def _():
                    act(
                        pltpu.make_async_copy(
                            arrived[m].at[picks_ref[count + k]], packed_ref.at[k], sems.at[k]
                        )
                    )

    each(lambda copy: copy.start())
    each(lambda copy: copy.wait())
    for k in range(count):
        widened = packed_ref[k].astype(jnp.float32)
        squares_ref[k] = jnp.sum(widened * widened, axis=-1, keepdims=True)


def place_tiles(picks, arrived, tile_rows):
    width = arrived[0].shape[1]
    blocks = [part.reshape(-1, tile_rows, width) for part in arrived]
    count = picks.shape[0] // 2
    limits = jnp.repeat(jnp.array([3, blocks[0].shape[0] - 1], jnp.int32), count)
    packed, squares = pl.pallas_call(
        place_kernel,
        in_specs=[pl.BlockSpec(memory_space=pltpu.SMEM)]
        + [pl.BlockSpec(memory_space=pl.ANY)] * 4,
        out_shape=[
            jax.ShapeDtypeStruct((count, tile_rows, width), arrived[0].dtype),
            jax.ShapeDtypeStruct((count, tile_rows, 1), jnp.float32),
        ],
        scratch_shapes=[pltpu.SemaphoreType.DMA((count,))],
        cost_estimate=pl.CostEstimate(
            flops=0, bytes_accessed=4 * count * tile_rows * width, transcendentals=0
        ),
    )(jnp.clip(picks, 0, limits), *blocks)
    return packed.reshape(-1, width), squares.reshape(-1, 1)


def ring_body(
    activations,
    tile_dest,
    segment_ids,
    norm_gain,
    q_weight,
    k_weight,
    v_weight,
    q_bias,
    k_bias,
    v_bias,
    o_weight,
):
    z = lax.axis_index("dp")
    y = lax.axis_index("groups")
    x = lax.axis_index("tensor")
    core = lax.axis_index("pair")
    t = x * 2 + core
    slots, tile_rows = tile_dest.shape[1], segment_ids.shape[2]
    width = activations.shape[1]
    rows = TPD * tile_rows
    peers = 2
    q_share = q_weight.shape[1] // 2

    kv_at = (core * 2 + y) * HEAD
    q_own = lax.dynamic_slice_in_dim(q_weight, y * q_share, q_share, 1)
    k_own = lax.dynamic_slice_in_dim(k_weight, kv_at, HEAD, 1)
    v_own = lax.dynamic_slice_in_dim(v_weight, kv_at, HEAD, 1)
    qkv_own = jnp.concatenate([q_own, k_own, v_own], axis=1)
    o_own = lax.dynamic_slice_in_dim(o_weight, y * q_share, q_share, 0)
    bias = jnp.concatenate(
        [
            lax.dynamic_slice_in_dim(q_bias, y * q_share, q_share, 0),
            lax.dynamic_slice_in_dim(k_bias, kv_at, HEAD, 0),
            lax.dynamic_slice_in_dim(v_bias, kv_at, HEAD, 0),
        ]
    ).astype(jnp.float32)[None, :]

    def hop(up, down):
        s = len(up)
        up.append(shift(up[-1], "dp", [(i, i + 1) for i in range(s - 1, 3)]))
        down.append(shift(down[-1], "dp", [(i + 1, i) for i in range(0, 4 - s)]))

    q_up, q_down = [qkv_own], [qkv_own]
    hop(q_up, q_down)

    own_plan = lax.dynamic_index_in_dim(tile_dest, z, 0, keepdims=False)
    slot_ids = jnp.arange(slots, dtype=jnp.int32)
    peer_ids = jnp.arange(peers, dtype=jnp.int32)
    partners = jnp.arange(4, dtype=jnp.int32) ^ z
    same_before = (own_plan[None, :] == own_plan[:, None]) & (slot_ids[None, :] < slot_ids[:, None])
    send_rank = jnp.sum(same_before.astype(jnp.int32), axis=1)
    chooser = (own_plan[None, None, :] == partners[:, None, None]) & (
        send_rank[None, None, :] == peer_ids[None, :, None]
    )
    send_slots = jnp.sum(chooser.astype(jnp.int32) * slot_ids, axis=2).reshape(-1)
    outgoing = pack_tiles(send_slots, activations, tile_rows)
    arrived = [outgoing[0]] + [
        shift(outgoing[m], "dp", [(i, i ^ m) for i in range(4)]) for m in range(1, 4)
    ]
    to_here = (tile_dest == z).astype(jnp.int32)
    from_each = jnp.sum(to_here, axis=1)
    first_place = jnp.cumsum(from_each) - from_each
    tile_ids = jnp.arange(TPD, dtype=jnp.int32)
    inside = (tile_ids[:, None] >= first_place[None, :]) & (
        tile_ids[:, None] < (first_place + from_each)[None, :]
    )
    source = jnp.sum(inside.astype(jnp.int32) * jnp.arange(4, dtype=jnp.int32)[None, :], axis=1)
    rank = jnp.sum(inside.astype(jnp.int32) * (tile_ids[:, None] - first_place[None, :]), axis=1)
    packed, squares = place_tiles(
        jnp.concatenate([source ^ z, rank]), arrived, tile_rows
    )
    flat_member = (tile_dest.reshape(-1) == z).astype(jnp.int32)
    flat_rank = jnp.cumsum(flat_member) - 1
    picker = flat_member[None, :] * (flat_rank[None, :] == tile_ids[:, None]).astype(jnp.int32)
    segment = jnp.sum(picker[:, :, None] * segment_ids.reshape(-1, tile_rows)[None, :, :], axis=1)
    positions = tile_positions(segment).reshape(rows, 1)
    positions = jnp.concatenate([positions, shift(positions, "groups", SWAP)], axis=0)
    half = HEAD // 2
    inverse = jnp.power(
        jnp.float32(1000000.0), -2.0 * jnp.arange(half, dtype=jnp.float32) / HEAD
    )
    angles = positions.astype(jnp.float32) * inverse[None, :]
    cosine, sine = jnp.cos(angles), jnp.sin(angles)
    cosine = jnp.concatenate([cosine, cosine], axis=1)
    sine = jnp.concatenate([-sine, sine], axis=1)

    packed, squares, q_up[1], q_down[1] = lax.optimization_barrier(
        (packed, squares, q_up[1], q_down[1])
    )
    hop(q_up, q_down)

    widened = packed.astype(jnp.float32)
    squares = squares + shift(squares, "pair", SWAP)
    squares = squares + shift(squares, "tensor", SWAP)
    gain = lax.dynamic_slice_in_dim(norm_gain, t * width, width, 0).astype(jnp.float32)
    normed = (widened * lax.rsqrt(squares / (4 * width) + norm_eps) * gain).astype(jnp.bfloat16)
    peer = shift(normed, "groups", SWAP)
    across_own = shift(normed, "tensor", SWAP)
    across_peer = shift(peer, "tensor", SWAP)
    q_up[2], q_down[2], peer, across_own, across_peer = lax.optimization_barrier(
        (q_up[2], q_down[2], peer, across_own, across_peer)
    )
    hop(q_up, q_down)
    here = jnp.concatenate([normed, peer], axis=0)
    across = jnp.concatenate([across_own, across_peer], axis=0)
    shares = [here, shift(here, "pair", SWAP), across, shift(across, "pair", SWAP)]
    *shares, o_own = lax.optimization_barrier((*shares, o_own))
    o_up, o_down = [o_own], [o_own]
    hop(o_up, o_down)

    def by_partner(up, down):
        first = jnp.where(z % 2 == 0, down[1], up[1])
        second = up[2] + down[2]
        third = jnp.where(z == 1, down[1], jnp.where(z == 2, up[1], up[3] + down[3]))
        return [up[0], first, second, third]

    q_blocks = by_partner(q_up[:3] + [q_up[2]], q_down[:3] + [q_down[2]])
    at = jnp.arange(4, dtype=jnp.int32) ^ z ^ t
    lin = linear_rows(at[:3], shares, q_blocks[:3])
    lin, q_up[3], q_down[3] = lax.optimization_barrier((lin, q_up[3], q_down[3]))
    context = attend_rows(
        shares, at[3], by_partner(q_up, q_down)[3], lin, bias, cosine, sine, positions, tile_rows
    )
    context, o_up[1], o_down[1] = lax.optimization_barrier((context, o_up[1], o_down[1]))
    hop(o_up, o_down)

    every = ("groups", "dp", "tensor", "pair")
    index = lambda zz, yy, xx, cc: ((yy * 4 + zz) * 2 + xx) * 2 + cc

    def project(block):
        return jnp.dot(context, block, preferred_element_type=jnp.float32)

    def to_chip(part, m, cores):
        pairs = []
        for zz in range(4):
            xd = (zz ^ m) // 2
            for cc in cores(zz):
                pairs += [(index(zz, i, 1 - xd, cc), index(zz, i, xd, cc)) for i in range(2)]
        return part + shift(part.astype(jnp.bfloat16), every, pairs).astype(jnp.float32)

    both = lambda zz: (0, 1)
    keeps_first = (z ^ core) % 2 == 0

    def halves(block):
        return jnp.split(block, 2, axis=1)

    def to_core(one, two):
        kept = project(jnp.where(keeps_first, one, two))
        sent = project(jnp.where(keeps_first, two, one)).astype(jnp.bfloat16)
        return kept + shift(sent, "pair", SWAP).astype(jnp.float32)

    def to_group(part):
        return part[:rows] + shift(part[rows:].astype(jnp.bfloat16), "groups", SWAP).astype(
            jnp.float32
        )

    o_first = jnp.where(z % 2 == 0, o_down[1], o_up[1])
    first = to_core(o_own, o_first)
    first, o_up[2], o_down[2] = lax.optimization_barrier((first, o_up[2], o_down[2]))
    hop(o_up, o_down)
    first = to_group(first)
    first, o_up[3], o_down[3] = lax.optimization_barrier((first, o_up[3], o_down[3]))
    first = to_chip(first, 0, both)
    o_blocks = by_partner(o_up, o_down)
    second = [
        to_group(to_core(one, two)) for one, two in zip(halves(o_blocks[2]), halves(o_blocks[3]))
    ]
    first, second[1] = lax.optimization_barrier((first, second[1]))
    second = jnp.concatenate([to_chip(part, 2, both) for part in second], axis=1)
    total = jnp.where(z // 2 == x, first, second)
    return (packed.astype(jnp.float32) + total).astype(jnp.bfloat16)


def solution(mesh):
    shape = dict(mesh.shape)
    ringed = shape == {"groups": 2, "dp": 4, "tensor": 2, "pair": 2}
    return jax.shard_map(
        ring_body if ringed else body,
        mesh=mesh,
        in_specs=(
            P(("groups", "dp"), ("tensor", "pair")),
            P("groups", None),
            P("groups", None, None),
            P(),
            P("dp", ("tensor", "pair")),
            P("dp", "tensor"),
            P("dp", "tensor"),
            P(("tensor", "pair")),
            P("tensor"),
            P("tensor"),
            P(("tensor", "pair"), "dp"),
        ),
        out_specs=P(("groups", "dp"), ("tensor", "pair")),
        check_vma=False,
    )
```

```python
import math

import jax
import jax.numpy as jnp
from jax import lax
from jax.experimental import pallas as pl
from jax.experimental.pallas import tpu as pltpu
from jax.sharding import PartitionSpec as P

QHEADS = 32
KVH = 8
HEAD = 128
TPD = 4
GROUP_SIZE = QHEADS // KVH


norm_eps = 1e-06

def normalize(values, gain_vector):
    widened = values.astype(jnp.float32)
    meansq = jnp.mean(widened * widened, axis=-1, keepdims=True)
    return (widened * lax.rsqrt(meansq + norm_eps) * gain_vector.astype(jnp.float32)).astype(
        jnp.bfloat16
    )


def rotary(values, positions):
    half_size = values.shape[-1] // 2
    inverse = jnp.power(
        jnp.float32(1000000.0), -2.0 * jnp.arange(half_size, dtype=jnp.float32) / values.shape[-1]
    )
    angles = positions.astype(jnp.float32)[:, None] * inverse[None, :]
    cosine = jnp.cos(angles)[:, None, :]
    sine_part = jnp.sin(angles)[:, None, :]
    front_half = values[..., :half_size]
    back_half = values[..., half_size:]
    return jnp.concatenate(
        [front_half * cosine - back_half * sine_part, back_half * cosine + front_half * sine_part],
        axis=-1,
    )


def tile_positions(segment):
    earlier = (segment[..., None, :] < segment[..., :, None]).astype(jnp.int32)
    first_row = jnp.sum(earlier, axis=-1)
    return jnp.arange(segment.shape[-1], dtype=jnp.int32) - first_row


def attend_tiles(query_groups, key_rows, value_rows, segment):
    tile_rows = query_groups.shape[1]
    scores = jnp.einsum(
        "tqgsd,tkgd->tgsqk", query_groups, key_rows, preferred_element_type=jnp.float32
    )
    scores = scores * (1.0 / math.sqrt(query_groups.shape[-1]))
    places = jnp.arange(tile_rows, dtype=jnp.int32)
    allowed = (segment[:, :, None] == segment[:, None, :]) & (
        places[None, None, :] <= places[None, :, None]
    )
    scores = jnp.where(allowed[:, None, None, :, :], scores, -1e30)
    attn_probs = jax.nn.softmax(scores, axis=-1).astype(jnp.bfloat16)
    context = jnp.einsum(
        "tgsqk,tkgd->tqgsd", attn_probs, value_rows, preferred_element_type=jnp.float32
    )
    return context.astype(jnp.bfloat16)


def body(
    activations,
    tile_dest,
    segment_ids,
    norm_gain,
    q_weight,
    k_weight,
    v_weight,
    q_bias,
    k_bias,
    v_bias,
    o_weight,
):
    dp_count = lax.axis_size("dp")
    own_index = lax.axis_index("dp")
    pair_size = lax.axis_size("pair")
    pair_index = lax.axis_index("pair")
    slot_count = tile_dest.shape[1]
    tile_rows = segment_ids.shape[2]
    feature_share = activations.shape[1]
    peer_slots = (slot_count + dp_count - 1) // dp_count
    own_plan = lax.dynamic_index_in_dim(tile_dest, own_index, 0, keepdims=False)
    slot_ids = jnp.arange(slot_count, dtype=jnp.int32)
    targets = jnp.arange(dp_count, dtype=jnp.int32)
    peer_ids = jnp.arange(peer_slots, dtype=jnp.int32)
    earlier_same = (own_plan[None, :] == own_plan[:, None]) & (
        slot_ids[None, :] < slot_ids[:, None]
    )
    send_rank = jnp.sum(earlier_same.astype(jnp.int32), axis=1)
    chooser = (own_plan[None, None, :] == targets[:, None, None]) & (
        send_rank[None, None, :] == peer_ids[None, :, None]
    )
    own_tiles = activations.reshape(slot_count, tile_rows, feature_share)
    outgoing = jnp.einsum(
        "jps,srf->jprf", chooser.astype(jnp.bfloat16), own_tiles, preferred_element_type=jnp.float32
    ).astype(jnp.bfloat16)
    arrived = lax.all_to_all(outgoing, "dp", split_axis=0, concat_axis=0, tiled=True)
    to_here = (tile_dest == own_index).astype(jnp.int32)
    from_each = jnp.sum(to_here, axis=1)
    first_place = jnp.cumsum(from_each) - from_each
    place_of = first_place[:, None] + peer_ids[None, :]
    landed = peer_ids[None, :] < from_each[:, None]
    tile_ids = jnp.arange(TPD, dtype=jnp.int32)
    placer = (place_of[None, :, :] == tile_ids[:, None, None]) & landed[None, :, :]
    packed_tiles = jnp.einsum(
        "ksp,sprf->krf", placer.astype(jnp.bfloat16), arrived, preferred_element_type=jnp.float32
    ).astype(jnp.bfloat16)
    row_count = TPD * tile_rows
    packed = packed_tiles.reshape(row_count, feature_share)
    flat_plan = tile_dest.reshape(-1)
    flat_member = (flat_plan == own_index).astype(jnp.int32)
    flat_rank = jnp.cumsum(flat_member) - 1
    picker = flat_member[None, :] * (flat_rank[None, :] == tile_ids[:, None]).astype(jnp.int32)
    flat_segments = segment_ids.reshape(-1, tile_rows)
    segment = jnp.sum(picker[:, :, None] * flat_segments[None, :, :], axis=1)
    positions = tile_positions(segment).reshape(row_count)
    whole_rows = lax.all_gather(packed, ("tensor", "pair"), axis=1, tiled=True)
    normed = normalize(whole_rows, norm_gain)
    q_width = q_weight.shape[1]
    kv_width = k_weight.shape[1]
    q_lin = jnp.dot(
        normed,
        lax.all_gather(q_weight, "dp", axis=0, tiled=True),
        preferred_element_type=jnp.float32,
    )
    k_lin = jnp.dot(
        normed,
        lax.all_gather(k_weight, "dp", axis=0, tiled=True),
        preferred_element_type=jnp.float32,
    )
    v_lin = jnp.dot(
        normed,
        lax.all_gather(v_weight, "dp", axis=0, tiled=True),
        preferred_element_type=jnp.float32,
    )
    q_heads = q_width // HEAD
    kv_heads = kv_width // HEAD
    queries = rotary(
        (q_lin + q_bias.astype(jnp.float32)).reshape(row_count, q_heads, HEAD), positions
    ).astype(jnp.bfloat16)
    keys_local = rotary(
        (k_lin + k_bias.astype(jnp.float32)).reshape(-1, kv_heads, HEAD), positions
    ).astype(jnp.bfloat16)
    values_local = (
        (v_lin + v_bias.astype(jnp.float32)).astype(jnp.bfloat16).reshape(-1, kv_heads, HEAD)
    )
    key_rows, value_rows = (keys_local, values_local)
    group_size = QHEADS // KVH
    kv_count = max(1, q_heads // group_size)
    group_span = q_heads // kv_count
    kv_first = pair_index * q_heads // group_size
    key_rows = lax.dynamic_slice_in_dim(key_rows, kv_first, kv_count, 1).reshape(
        TPD, tile_rows, kv_count, HEAD
    )
    value_rows = lax.dynamic_slice_in_dim(value_rows, kv_first, kv_count, 1).reshape(
        TPD, tile_rows, kv_count, HEAD
    )
    query_groups = queries.reshape(TPD, tile_rows, kv_count, group_span, HEAD)
    context = attend_tiles(query_groups, key_rows, value_rows, segment).reshape(
        row_count, q_heads * HEAD
    )
    partials = jnp.dot(
        context,
        lax.all_gather(o_weight, "dp", axis=1, tiled=True),
        preferred_element_type=jnp.float32,
    )
    full_sums = lax.psum(partials.astype(jnp.bfloat16), ("tensor", "pair")).astype(jnp.float32)
    my_slot = lax.axis_index("tensor") * pair_size + pair_index
    summed = lax.dynamic_slice_in_dim(full_sums, my_slot * feature_share, feature_share, 1)
    return (packed.astype(jnp.float32) + summed).astype(jnp.bfloat16)


def shift(values, axis, pairs):
    return lax.ppermute(values, axis, pairs)


SWAP = [(0, 1), (1, 0)]


def fetch_share(which, shares, target, sem):
    def each(act):
        for k, share in enumerate(shares):

            @pl.when(which == k)
            def _():
                act(pltpu.make_async_copy(share, target, sem))

    return each


def linear_kernel(at_ref, *refs):
    shares, blocks = refs[:4], refs[4:7]
    out_ref, share_buf, block_buf, sems = refs[7:]
    fetches = []
    for m in range(3):
        fetches.append(fetch_share(at_ref[m], shares, share_buf.at[m], sems.at[m]))
        fetches[m](lambda copy: copy.start())
        pltpu.make_async_copy(blocks[m], block_buf.at[m], sems.at[3 + m]).start()
    for m in range(3):
        fetches[m](lambda copy: copy.wait())
        pltpu.make_async_copy(blocks[m], block_buf.at[m], sems.at[3 + m]).wait()
    step = 128

    @pl.loop(0, out_ref.shape[0] // step)
    def _(i):
        at = pl.ds(pl.multiple_of(i * step, step), step)
        total = None
        for m in range(3):
            part = jnp.dot(share_buf[m, at], block_buf[m], preferred_element_type=jnp.float32)
            total = part if total is None else total + part
        out_ref[at] = total


def linear_rows(at, shares, blocks):
    (count, depth), width = shares[0].shape, blocks[0].shape[1]
    return pl.pallas_call(
        linear_kernel,
        in_specs=[pl.BlockSpec(memory_space=pltpu.SMEM)]
        + [pl.BlockSpec(memory_space=pl.ANY)] * 7,
        out_specs=pl.BlockSpec(memory_space=pltpu.VMEM),
        out_shape=jax.ShapeDtypeStruct((count, width), jnp.float32),
        scratch_shapes=[
            pltpu.VMEM((3, count, depth), jnp.bfloat16),
            pltpu.VMEM((3, depth, width), jnp.bfloat16),
            pltpu.SemaphoreType.DMA((6,)),
        ],
        compiler_params=pltpu.CompilerParams(vmem_limit_bytes=32 * 1024 * 1024),
    )(at, *shares, *blocks)


def attention_kernel(at_ref, *refs):
    shares, refs = refs[:4], refs[4:]
    block_ref, lin_ref, bias_ref, cos_ref, sin_ref, pos_ref, out_ref, share_buf, sem = refs
    step = pl.program_id(0)

    @pl.when(step == 0)
    def _():
        fetch = fetch_share(at_ref[0], shares, share_buf, sem)
        fetch(lambda copy: copy.start())
        fetch(lambda copy: copy.wait())

    own = pl.ds(pl.multiple_of(step * lin_ref.shape[0], lin_ref.shape[0]), lin_ref.shape[0])

    heads = out_ref.shape[1] // HEAD
    rows = lin_ref.shape[0]
    lin = lin_ref[...] + jnp.dot(
        share_buf[own], block_ref[...], preferred_element_type=jnp.float32
    )
    lin = lin + bias_ref[...]
    cosine = cos_ref[...]
    sine = sin_ref[...]

    def rotate(values):
        return (values * cosine + pltpu.roll(values, HEAD // 2, 1) * sine).astype(jnp.bfloat16)

    queries = jnp.concatenate(
        [rotate(lin[:, h * HEAD : (h + 1) * HEAD]) for h in range(heads)], axis=0
    )
    keys = rotate(lin[:, heads * HEAD : (heads + 1) * HEAD])
    value_rows = lin[:, (heads + 1) * HEAD :].astype(jnp.bfloat16)
    scores = lax.dot_general(
        queries, keys, (((1,), (1,)), ((), ())), preferred_element_type=jnp.float32
    )
    scores = (scores * (1.0 / math.sqrt(HEAD))).reshape(heads, rows, rows)
    row = lax.broadcasted_iota(jnp.int32, (rows, rows), 0)
    column = lax.broadcasted_iota(jnp.int32, (rows, rows), 1)
    allowed = (column <= row) & (column >= row - pos_ref[...])
    scores = jnp.where(allowed[None], scores, -1e30)
    largest = jnp.max(scores, axis=-1, keepdims=True)
    weights = jnp.exp(scores - largest)
    probs = (weights / jnp.sum(weights, axis=-1, keepdims=True)).astype(jnp.bfloat16)
    context = lax.dot_general(
        probs.reshape(heads * rows, rows),
        value_rows,
        (((1,), (0,)), ((), ())),
        preferred_element_type=jnp.float32,
    ).astype(jnp.bfloat16)
    for h in range(heads):
        out_ref[:, h * HEAD : (h + 1) * HEAD] = context[h * rows : (h + 1) * rows]


def attend_rows(shares, at, block, lin, bias, cosine, sine, positions, tile_rows):
    count, width = lin.shape
    out_width = width - 2 * HEAD
    by_tile = lambda w: pl.BlockSpec((tile_rows, w), lambda i, at: (i, 0))
    return pl.pallas_call(
        attention_kernel,
        grid_spec=pltpu.PrefetchScalarGridSpec(
            num_scalar_prefetch=1,
            grid=(count // tile_rows,),
            in_specs=[
                *[pl.BlockSpec(memory_space=pl.ANY)] * 4,
                pl.BlockSpec(block.shape, lambda i, at: (0, 0)),
                by_tile(width),
                pl.BlockSpec((1, width), lambda i, at: (0, 0)),
                by_tile(HEAD),
                by_tile(HEAD),
                by_tile(1),
            ],
            out_specs=by_tile(out_width),
            scratch_shapes=[
                pltpu.VMEM(shares[0].shape, jnp.bfloat16),
                pltpu.SemaphoreType.DMA(()),
            ],
        ),
        out_shape=jax.ShapeDtypeStruct((count, out_width), jnp.bfloat16),
        compiler_params=pltpu.CompilerParams(vmem_limit_bytes=32 * 1024 * 1024),
    )(at.reshape(1), *shares, block, lin, bias, cosine, sine, positions)


def pack_kernel(slots_ref, *refs):
    for m in range(4):
        refs[4 + m][...] = refs[m][...]


def pack_tiles(send_slots, activations, tile_rows):
    width = activations.shape[1]
    tiles = activations.reshape(-1, tile_rows, width)
    peers = send_slots.shape[0] // 4
    block = (1, tile_rows, width)
    pick = lambda m: pl.BlockSpec(block, lambda p, slots: (slots[m * peers + p], 0, 0))
    outs = pl.pallas_call(
        pack_kernel,
        grid_spec=pltpu.PrefetchScalarGridSpec(
            num_scalar_prefetch=1,
            grid=(peers,),
            in_specs=[pick(m) for m in range(4)],
            out_specs=[pl.BlockSpec(block, lambda p, slots: (p, 0, 0))] * 4,
        ),
        out_shape=[jax.ShapeDtypeStruct((peers, tile_rows, width), activations.dtype)] * 4,
        cost_estimate=pl.CostEstimate(
            flops=0, bytes_accessed=4 * activations.size, transcendentals=0
        ),
    )(jnp.clip(send_slots, 0, tiles.shape[0] - 1), *[tiles] * 4)
    return [out.reshape(peers * tile_rows, width) for out in outs]


def place_kernel(picks_ref, *refs):
    arrived, (packed_ref, squares_ref, sems) = refs[:4], refs[4:]
    count = packed_ref.shape[0]

    def each(act):
        for k in range(count):
            for m in range(4):

                @pl.when(picks_ref[k] == m)
                def _():
                    act(
                        pltpu.make_async_copy(
                            arrived[m].at[picks_ref[count + k]], packed_ref.at[k], sems.at[k]
                        )
                    )

    each(lambda copy: copy.start())
    each(lambda copy: copy.wait())
    for k in range(count):
        widened = packed_ref[k].astype(jnp.float32)
        squares_ref[k] = jnp.sum(widened * widened, axis=-1, keepdims=True)


def place_tiles(picks, arrived, tile_rows):
    width = arrived[0].shape[1]
    blocks = [part.reshape(-1, tile_rows, width) for part in arrived]
    count = picks.shape[0] // 2
    limits = jnp.repeat(jnp.array([3, blocks[0].shape[0] - 1], jnp.int32), count)
    packed, squares = pl.pallas_call(
        place_kernel,
        in_specs=[pl.BlockSpec(memory_space=pltpu.SMEM)]
        + [pl.BlockSpec(memory_space=pl.ANY)] * 4,
        out_shape=[
            jax.ShapeDtypeStruct((count, tile_rows, width), arrived[0].dtype),
            jax.ShapeDtypeStruct((count, tile_rows, 1), jnp.float32),
        ],
        scratch_shapes=[pltpu.SemaphoreType.DMA((count,))],
        cost_estimate=pl.CostEstimate(
            flops=0, bytes_accessed=4 * count * tile_rows * width, transcendentals=0
        ),
    )(jnp.clip(picks, 0, limits), *blocks)
    return packed.reshape(-1, width), squares.reshape(-1, 1)


def ring_body(
    activations,
    tile_dest,
    segment_ids,
    norm_gain,
    q_weight,
    k_weight,
    v_weight,
    q_bias,
    k_bias,
    v_bias,
    o_weight,
):
    z = lax.axis_index("dp")
    y = lax.axis_index("groups")
    x = lax.axis_index("tensor")
    core = lax.axis_index("pair")
    t = x * 2 + core
    slots, tile_rows = tile_dest.shape[1], segment_ids.shape[2]
    width = activations.shape[1]
    rows = TPD * tile_rows
    peers = 2
    q_share = q_weight.shape[1] // 2

    kv_at = (core * 2 + y) * HEAD
    q_own = lax.dynamic_slice_in_dim(q_weight, y * q_share, q_share, 1)
    k_own = lax.dynamic_slice_in_dim(k_weight, kv_at, HEAD, 1)
    v_own = lax.dynamic_slice_in_dim(v_weight, kv_at, HEAD, 1)
    qkv_own = jnp.concatenate([q_own, k_own, v_own], axis=1)
    o_own = lax.dynamic_slice_in_dim(o_weight, y * q_share, q_share, 0)
    bias = jnp.concatenate(
        [
            lax.dynamic_slice_in_dim(q_bias, y * q_share, q_share, 0),
            lax.dynamic_slice_in_dim(k_bias, kv_at, HEAD, 0),
            lax.dynamic_slice_in_dim(v_bias, kv_at, HEAD, 0),
        ]
    ).astype(jnp.float32)[None, :]

    def hop(up, down):
        s = len(up)
        up.append(shift(up[-1], "dp", [(i, i + 1) for i in range(s - 1, 3)]))
        down.append(shift(down[-1], "dp", [(i + 1, i) for i in range(0, 4 - s)]))

    q_up, q_down = [qkv_own], [qkv_own]
    hop(q_up, q_down)

    own_plan = lax.dynamic_index_in_dim(tile_dest, z, 0, keepdims=False)
    slot_ids = jnp.arange(slots, dtype=jnp.int32)
    peer_ids = jnp.arange(peers, dtype=jnp.int32)
    partners = jnp.arange(4, dtype=jnp.int32) ^ z
    same_before = (own_plan[None, :] == own_plan[:, None]) & (slot_ids[None, :] < slot_ids[:, None])
    send_rank = jnp.sum(same_before.astype(jnp.int32), axis=1)
    chooser = (own_plan[None, None, :] == partners[:, None, None]) & (
        send_rank[None, None, :] == peer_ids[None, :, None]
    )
    send_slots = jnp.sum(chooser.astype(jnp.int32) * slot_ids, axis=2).reshape(-1)
    outgoing = pack_tiles(send_slots, activations, tile_rows)
    arrived = [outgoing[0]] + [
        shift(outgoing[m], "dp", [(i, i ^ m) for i in range(4)]) for m in range(1, 4)
    ]
    *arrived, q_up[1], q_down[1] = lax.optimization_barrier((*arrived, q_up[1], q_down[1]))
    hop(q_up, q_down)
    to_here = (tile_dest == z).astype(jnp.int32)
    from_each = jnp.sum(to_here, axis=1)
    first_place = jnp.cumsum(from_each) - from_each
    tile_ids = jnp.arange(TPD, dtype=jnp.int32)
    inside = (tile_ids[:, None] >= first_place[None, :]) & (
        tile_ids[:, None] < (first_place + from_each)[None, :]
    )
    source = jnp.sum(inside.astype(jnp.int32) * jnp.arange(4, dtype=jnp.int32)[None, :], axis=1)
    rank = jnp.sum(inside.astype(jnp.int32) * (tile_ids[:, None] - first_place[None, :]), axis=1)
    packed, squares = place_tiles(
        jnp.concatenate([source ^ z, rank]), arrived, tile_rows
    )
    flat_member = (tile_dest.reshape(-1) == z).astype(jnp.int32)
    flat_rank = jnp.cumsum(flat_member) - 1
    picker = flat_member[None, :] * (flat_rank[None, :] == tile_ids[:, None]).astype(jnp.int32)
    segment = jnp.sum(picker[:, :, None] * segment_ids.reshape(-1, tile_rows)[None, :, :], axis=1)
    positions = tile_positions(segment).reshape(rows, 1)
    positions = jnp.concatenate([positions, shift(positions, "groups", SWAP)], axis=0)
    half = HEAD // 2
    inverse = jnp.power(
        jnp.float32(1000000.0), -2.0 * jnp.arange(half, dtype=jnp.float32) / HEAD
    )
    angles = positions.astype(jnp.float32) * inverse[None, :]
    cosine, sine = jnp.cos(angles), jnp.sin(angles)
    cosine = jnp.concatenate([cosine, cosine], axis=1)
    sine = jnp.concatenate([-sine, sine], axis=1)

    widened = packed.astype(jnp.float32)
    squares = squares + shift(squares, "pair", SWAP)
    squares = squares + shift(squares, "tensor", SWAP)
    gain = lax.dynamic_slice_in_dim(norm_gain, t * width, width, 0).astype(jnp.float32)
    normed = (widened * lax.rsqrt(squares / (4 * width) + norm_eps) * gain).astype(jnp.bfloat16)
    peer = shift(normed, "groups", SWAP)
    across_own = shift(normed, "tensor", SWAP)
    q_up[2], q_down[2], peer, across_own = lax.optimization_barrier(
        (q_up[2], q_down[2], peer, across_own)
    )
    hop(q_up, q_down)
    here = jnp.concatenate([normed, peer], axis=0)
    here_other, across_peer = shift(here, "pair", SWAP), shift(peer, "tensor", SWAP)
    here_other, across_peer, o_own, q_up[3], q_down[3] = lax.optimization_barrier(
        (here_other, across_peer, o_own, q_up[3], q_down[3])
    )
    across = jnp.concatenate([across_own, across_peer], axis=0)
    shares = [here, here_other, across, shift(across, "pair", SWAP)]
    o_up, o_down = [o_own], [o_own]
    hop(o_up, o_down)

    def by_partner(up, down):
        first = jnp.where(z % 2 == 0, down[1], up[1])
        second = up[2] + down[2]
        third = jnp.where(z == 1, down[1], jnp.where(z == 2, up[1], up[3] + down[3]))
        return [up[0], first, second, third]

    q_blocks = by_partner(q_up[:3] + [q_up[2]], q_down[:3] + [q_down[2]])
    at = jnp.arange(4, dtype=jnp.int32) ^ z ^ t
    lin = linear_rows(at[:3], shares, q_blocks[:3])
    context = attend_rows(
        shares, at[3], by_partner(q_up, q_down)[3], lin, bias, cosine, sine, positions, tile_rows
    )
    context, o_up[1], o_down[1] = lax.optimization_barrier((context, o_up[1], o_down[1]))
    hop(o_up, o_down)

    every = ("groups", "dp", "tensor", "pair")
    index = lambda zz, yy, xx, cc: ((yy * 4 + zz) * 2 + xx) * 2 + cc

    def project(block):
        return jnp.dot(context, block, preferred_element_type=jnp.float32)

    def to_chip(part, m, cores):
        pairs = []
        for zz in range(4):
            xd = (zz ^ m) // 2
            for cc in cores(zz):
                pairs += [(index(zz, i, 1 - xd, cc), index(zz, i, xd, cc)) for i in range(2)]
        return part + shift(part.astype(jnp.bfloat16), every, pairs).astype(jnp.float32)

    both = lambda zz: (0, 1)
    keeps_first = (z ^ core) % 2 == 0

    def halves(block):
        return jnp.split(block, 2, axis=1)

    def to_core(one, two):
        kept = project(jnp.where(keeps_first, one, two))
        sent = project(jnp.where(keeps_first, two, one)).astype(jnp.bfloat16)
        return kept + shift(sent, "pair", SWAP).astype(jnp.float32)

    def to_group(part):
        return part[:rows] + shift(part[rows:].astype(jnp.bfloat16), "groups", SWAP).astype(
            jnp.float32
        )

    o_first = jnp.where(z % 2 == 0, o_down[1], o_up[1])
    first = to_core(o_own, o_first)
    first, o_up[2], o_down[2] = lax.optimization_barrier((first, o_up[2], o_down[2]))
    hop(o_up, o_down)
    first = to_group(first)
    first, o_up[3], o_down[3] = lax.optimization_barrier((first, o_up[3], o_down[3]))
    first = to_chip(first, 0, both)
    o_blocks = by_partner(o_up, o_down)
    second = [
        to_group(to_core(one, two)) for one, two in zip(halves(o_blocks[2]), halves(o_blocks[3]))
    ]
    first, second[1] = lax.optimization_barrier((first, second[1]))
    second = jnp.concatenate([to_chip(part, 2, both) for part in second], axis=1)
    total = jnp.where(z // 2 == x, first, second)
    return (packed.astype(jnp.float32) + total).astype(jnp.bfloat16)


def solution(mesh):
    shape = dict(mesh.shape)
    ringed = shape == {"groups": 2, "dp": 4, "tensor": 2, "pair": 2}
    return jax.shard_map(
        ring_body if ringed else body,
        mesh=mesh,
        in_specs=(
            P(("groups", "dp"), ("tensor", "pair")),
            P("groups", None),
            P("groups", None, None),
            P(),
            P("dp", ("tensor", "pair")),
            P("dp", "tensor"),
            P("dp", "tensor"),
            P(("tensor", "pair")),
            P("tensor"),
            P("tensor"),
            P(("tensor", "pair"), "dp"),
        ),
        out_specs=P(("groups", "dp"), ("tensor", "pair")),
        check_vma=False,
    )
```

```python
import math

import jax
import jax.numpy as jnp
from jax import lax
from jax.experimental import pallas as pl
from jax.experimental.pallas import tpu as pltpu
from jax.sharding import PartitionSpec as P

QHEADS = 32
KVH = 8
HEAD = 128
TPD = 4
GROUP_SIZE = QHEADS // KVH


norm_eps = 1e-06

def normalize(values, gain_vector):
    widened = values.astype(jnp.float32)
    meansq = jnp.mean(widened * widened, axis=-1, keepdims=True)
    return (widened * lax.rsqrt(meansq + norm_eps) * gain_vector.astype(jnp.float32)).astype(
        jnp.bfloat16
    )


def rotary(values, positions):
    half_size = values.shape[-1] // 2
    inverse = jnp.power(
        jnp.float32(1000000.0), -2.0 * jnp.arange(half_size, dtype=jnp.float32) / values.shape[-1]
    )
    angles = positions.astype(jnp.float32)[:, None] * inverse[None, :]
    cosine = jnp.cos(angles)[:, None, :]
    sine_part = jnp.sin(angles)[:, None, :]
    front_half = values[..., :half_size]
    back_half = values[..., half_size:]
    return jnp.concatenate(
        [front_half * cosine - back_half * sine_part, back_half * cosine + front_half * sine_part],
        axis=-1,
    )


def tile_positions(segment):
    earlier = (segment[..., None, :] < segment[..., :, None]).astype(jnp.int32)
    first_row = jnp.sum(earlier, axis=-1)
    return jnp.arange(segment.shape[-1], dtype=jnp.int32) - first_row


def attend_tiles(query_groups, key_rows, value_rows, segment):
    tile_rows = query_groups.shape[1]
    scores = jnp.einsum(
        "tqgsd,tkgd->tgsqk", query_groups, key_rows, preferred_element_type=jnp.float32
    )
    scores = scores * (1.0 / math.sqrt(query_groups.shape[-1]))
    places = jnp.arange(tile_rows, dtype=jnp.int32)
    allowed = (segment[:, :, None] == segment[:, None, :]) & (
        places[None, None, :] <= places[None, :, None]
    )
    scores = jnp.where(allowed[:, None, None, :, :], scores, -1e30)
    attn_probs = jax.nn.softmax(scores, axis=-1).astype(jnp.bfloat16)
    context = jnp.einsum(
        "tgsqk,tkgd->tqgsd", attn_probs, value_rows, preferred_element_type=jnp.float32
    )
    return context.astype(jnp.bfloat16)


def body(
    activations,
    tile_dest,
    segment_ids,
    norm_gain,
    q_weight,
    k_weight,
    v_weight,
    q_bias,
    k_bias,
    v_bias,
    o_weight,
):
    dp_count = lax.axis_size("dp")
    own_index = lax.axis_index("dp")
    pair_size = lax.axis_size("pair")
    pair_index = lax.axis_index("pair")
    slot_count = tile_dest.shape[1]
    tile_rows = segment_ids.shape[2]
    feature_share = activations.shape[1]
    peer_slots = (slot_count + dp_count - 1) // dp_count
    own_plan = lax.dynamic_index_in_dim(tile_dest, own_index, 0, keepdims=False)
    slot_ids = jnp.arange(slot_count, dtype=jnp.int32)
    targets = jnp.arange(dp_count, dtype=jnp.int32)
    peer_ids = jnp.arange(peer_slots, dtype=jnp.int32)
    earlier_same = (own_plan[None, :] == own_plan[:, None]) & (
        slot_ids[None, :] < slot_ids[:, None]
    )
    send_rank = jnp.sum(earlier_same.astype(jnp.int32), axis=1)
    chooser = (own_plan[None, None, :] == targets[:, None, None]) & (
        send_rank[None, None, :] == peer_ids[None, :, None]
    )
    own_tiles = activations.reshape(slot_count, tile_rows, feature_share)
    outgoing = jnp.einsum(
        "jps,srf->jprf", chooser.astype(jnp.bfloat16), own_tiles, preferred_element_type=jnp.float32
    ).astype(jnp.bfloat16)
    arrived = lax.all_to_all(outgoing, "dp", split_axis=0, concat_axis=0, tiled=True)
    to_here = (tile_dest == own_index).astype(jnp.int32)
    from_each = jnp.sum(to_here, axis=1)
    first_place = jnp.cumsum(from_each) - from_each
    place_of = first_place[:, None] + peer_ids[None, :]
    landed = peer_ids[None, :] < from_each[:, None]
    tile_ids = jnp.arange(TPD, dtype=jnp.int32)
    placer = (place_of[None, :, :] == tile_ids[:, None, None]) & landed[None, :, :]
    packed_tiles = jnp.einsum(
        "ksp,sprf->krf", placer.astype(jnp.bfloat16), arrived, preferred_element_type=jnp.float32
    ).astype(jnp.bfloat16)
    row_count = TPD * tile_rows
    packed = packed_tiles.reshape(row_count, feature_share)
    flat_plan = tile_dest.reshape(-1)
    flat_member = (flat_plan == own_index).astype(jnp.int32)
    flat_rank = jnp.cumsum(flat_member) - 1
    picker = flat_member[None, :] * (flat_rank[None, :] == tile_ids[:, None]).astype(jnp.int32)
    flat_segments = segment_ids.reshape(-1, tile_rows)
    segment = jnp.sum(picker[:, :, None] * flat_segments[None, :, :], axis=1)
    positions = tile_positions(segment).reshape(row_count)
    whole_rows = lax.all_gather(packed, ("tensor", "pair"), axis=1, tiled=True)
    normed = normalize(whole_rows, norm_gain)
    q_width = q_weight.shape[1]
    kv_width = k_weight.shape[1]
    q_lin = jnp.dot(
        normed,
        lax.all_gather(q_weight, "dp", axis=0, tiled=True),
        preferred_element_type=jnp.float32,
    )
    k_lin = jnp.dot(
        normed,
        lax.all_gather(k_weight, "dp", axis=0, tiled=True),
        preferred_element_type=jnp.float32,
    )
    v_lin = jnp.dot(
        normed,
        lax.all_gather(v_weight, "dp", axis=0, tiled=True),
        preferred_element_type=jnp.float32,
    )
    q_heads = q_width // HEAD
    kv_heads = kv_width // HEAD
    queries = rotary(
        (q_lin + q_bias.astype(jnp.float32)).reshape(row_count, q_heads, HEAD), positions
    ).astype(jnp.bfloat16)
    keys_local = rotary(
        (k_lin + k_bias.astype(jnp.float32)).reshape(-1, kv_heads, HEAD), positions
    ).astype(jnp.bfloat16)
    values_local = (
        (v_lin + v_bias.astype(jnp.float32)).astype(jnp.bfloat16).reshape(-1, kv_heads, HEAD)
    )
    key_rows, value_rows = (keys_local, values_local)
    group_size = QHEADS // KVH
    kv_count = max(1, q_heads // group_size)
    group_span = q_heads // kv_count
    kv_first = pair_index * q_heads // group_size
    key_rows = lax.dynamic_slice_in_dim(key_rows, kv_first, kv_count, 1).reshape(
        TPD, tile_rows, kv_count, HEAD
    )
    value_rows = lax.dynamic_slice_in_dim(value_rows, kv_first, kv_count, 1).reshape(
        TPD, tile_rows, kv_count, HEAD
    )
    query_groups = queries.reshape(TPD, tile_rows, kv_count, group_span, HEAD)
    context = attend_tiles(query_groups, key_rows, value_rows, segment).reshape(
        row_count, q_heads * HEAD
    )
    partials = jnp.dot(
        context,
        lax.all_gather(o_weight, "dp", axis=1, tiled=True),
        preferred_element_type=jnp.float32,
    )
    full_sums = lax.psum(partials.astype(jnp.bfloat16), ("tensor", "pair")).astype(jnp.float32)
    my_slot = lax.axis_index("tensor") * pair_size + pair_index
    summed = lax.dynamic_slice_in_dim(full_sums, my_slot * feature_share, feature_share, 1)
    return (packed.astype(jnp.float32) + summed).astype(jnp.bfloat16)


def shift(values, axis, pairs):
    return lax.ppermute(values, axis, pairs)


SWAP = [(0, 1), (1, 0)]


def fetch_share(which, shares, target, sem):
    def each(act):
        for k, share in enumerate(shares):

            @pl.when(which == k)
            def _():
                act(pltpu.make_async_copy(share, target, sem))

    return each


def linear_kernel(at_ref, *refs):
    shares, blocks = refs[:4], refs[4:7]
    out_ref, share_buf, block_buf, sems = refs[7:]
    fetches = []
    for m in range(3):
        fetches.append(fetch_share(at_ref[m], shares, share_buf.at[m], sems.at[m]))
        fetches[m](lambda copy: copy.start())
        pltpu.make_async_copy(blocks[m], block_buf.at[m], sems.at[3 + m]).start()
    for m in range(3):
        fetches[m](lambda copy: copy.wait())
        pltpu.make_async_copy(blocks[m], block_buf.at[m], sems.at[3 + m]).wait()
    step = 128

    @pl.loop(0, out_ref.shape[0] // step)
    def _(i):
        at = pl.ds(pl.multiple_of(i * step, step), step)
        total = None
        for m in range(3):
            part = jnp.dot(share_buf[m, at], block_buf[m], preferred_element_type=jnp.float32)
            total = part if total is None else total + part
        out_ref[at] = total


def linear_rows(at, shares, blocks):
    (count, depth), width = shares[0].shape, blocks[0].shape[1]
    return pl.pallas_call(
        linear_kernel,
        in_specs=[pl.BlockSpec(memory_space=pltpu.SMEM)]
        + [pl.BlockSpec(memory_space=pl.ANY)] * 7,
        out_specs=pl.BlockSpec(memory_space=pltpu.VMEM),
        out_shape=jax.ShapeDtypeStruct((count, width), jnp.float32),
        scratch_shapes=[
            pltpu.VMEM((3, count, depth), jnp.bfloat16),
            pltpu.VMEM((3, depth, width), jnp.bfloat16),
            pltpu.SemaphoreType.DMA((6,)),
        ],
        compiler_params=pltpu.CompilerParams(vmem_limit_bytes=32 * 1024 * 1024),
    )(at, *shares, *blocks)


def attention_kernel(at_ref, *refs):
    shares, refs = refs[:4], refs[4:]
    block_ref, lin_ref, bias_ref, cos_ref, sin_ref, pos_ref, out_ref, share_buf, sem = refs
    step = pl.program_id(0)

    @pl.when(step == 0)
    def _():
        fetch = fetch_share(at_ref[0], shares, share_buf, sem)
        fetch(lambda copy: copy.start())
        fetch(lambda copy: copy.wait())

    own = pl.ds(pl.multiple_of(step * lin_ref.shape[0], lin_ref.shape[0]), lin_ref.shape[0])

    heads = out_ref.shape[1] // HEAD
    rows = lin_ref.shape[0]
    lin = lin_ref[...] + jnp.dot(
        share_buf[own], block_ref[...], preferred_element_type=jnp.float32
    )
    lin = lin + bias_ref[...]
    cosine = cos_ref[...]
    sine = sin_ref[...]

    def rotate(values):
        return (values * cosine + pltpu.roll(values, HEAD // 2, 1) * sine).astype(jnp.bfloat16)

    queries = jnp.concatenate(
        [rotate(lin[:, h * HEAD : (h + 1) * HEAD]) for h in range(heads)], axis=0
    )
    keys = rotate(lin[:, heads * HEAD : (heads + 1) * HEAD])
    value_rows = lin[:, (heads + 1) * HEAD :].astype(jnp.bfloat16)
    scores = lax.dot_general(
        queries, keys, (((1,), (1,)), ((), ())), preferred_element_type=jnp.float32
    )
    scores = (scores * (1.0 / math.sqrt(HEAD))).reshape(heads, rows, rows)
    row = lax.broadcasted_iota(jnp.int32, (rows, rows), 0)
    column = lax.broadcasted_iota(jnp.int32, (rows, rows), 1)
    allowed = (column <= row) & (column >= row - pos_ref[...])
    scores = jnp.where(allowed[None], scores, -1e30)
    largest = jnp.max(scores, axis=-1, keepdims=True)
    weights = jnp.exp(scores - largest)
    probs = (weights / jnp.sum(weights, axis=-1, keepdims=True)).astype(jnp.bfloat16)
    context = lax.dot_general(
        probs.reshape(heads * rows, rows),
        value_rows,
        (((1,), (0,)), ((), ())),
        preferred_element_type=jnp.float32,
    ).astype(jnp.bfloat16)
    for h in range(heads):
        out_ref[:, h * HEAD : (h + 1) * HEAD] = context[h * rows : (h + 1) * rows]


def attend_rows(shares, at, block, lin, bias, cosine, sine, positions, tile_rows):
    count, width = lin.shape
    out_width = width - 2 * HEAD
    by_tile = lambda w: pl.BlockSpec((tile_rows, w), lambda i, at: (i, 0))
    return pl.pallas_call(
        attention_kernel,
        grid_spec=pltpu.PrefetchScalarGridSpec(
            num_scalar_prefetch=1,
            grid=(count // tile_rows,),
            in_specs=[
                *[pl.BlockSpec(memory_space=pl.ANY)] * 4,
                pl.BlockSpec(block.shape, lambda i, at: (0, 0)),
                by_tile(width),
                pl.BlockSpec((1, width), lambda i, at: (0, 0)),
                by_tile(HEAD),
                by_tile(HEAD),
                by_tile(1),
            ],
            out_specs=by_tile(out_width),
            scratch_shapes=[
                pltpu.VMEM(shares[0].shape, jnp.bfloat16),
                pltpu.SemaphoreType.DMA(()),
            ],
        ),
        out_shape=jax.ShapeDtypeStruct((count, out_width), jnp.bfloat16),
        compiler_params=pltpu.CompilerParams(vmem_limit_bytes=32 * 1024 * 1024),
    )(at.reshape(1), *shares, block, lin, bias, cosine, sine, positions)


def pack_kernel(slots_ref, *refs):
    for m in range(4):
        refs[4 + m][...] = refs[m][...]


def pack_tiles(send_slots, activations, tile_rows):
    width = activations.shape[1]
    tiles = activations.reshape(-1, tile_rows, width)
    peers = send_slots.shape[0] // 4
    block = (1, tile_rows, width)
    pick = lambda m: pl.BlockSpec(block, lambda p, slots: (slots[m * peers + p], 0, 0))
    outs = pl.pallas_call(
        pack_kernel,
        grid_spec=pltpu.PrefetchScalarGridSpec(
            num_scalar_prefetch=1,
            grid=(peers,),
            in_specs=[pick(m) for m in range(4)],
            out_specs=[pl.BlockSpec(block, lambda p, slots: (p, 0, 0))] * 4,
        ),
        out_shape=[jax.ShapeDtypeStruct((peers, tile_rows, width), activations.dtype)] * 4,
        cost_estimate=pl.CostEstimate(
            flops=0, bytes_accessed=4 * activations.size, transcendentals=0
        ),
    )(jnp.clip(send_slots, 0, tiles.shape[0] - 1), *[tiles] * 4)
    return [out.reshape(peers * tile_rows, width) for out in outs]


def place_kernel(picks_ref, *refs):
    arrived, (packed_ref, squares_ref, sems) = refs[:4], refs[4:]
    count = packed_ref.shape[0]

    def each(act):
        for k in range(count):
            for m in range(4):

                @pl.when(picks_ref[k] == m)
                def _():
                    act(
                        pltpu.make_async_copy(
                            arrived[m].at[picks_ref[count + k]], packed_ref.at[k], sems.at[k]
                        )
                    )

    each(lambda copy: copy.start())
    each(lambda copy: copy.wait())
    for k in range(count):
        widened = packed_ref[k].astype(jnp.float32)
        squares_ref[k] = jnp.sum(widened * widened, axis=-1, keepdims=True)


def place_tiles(picks, arrived, tile_rows):
    width = arrived[0].shape[1]
    blocks = [part.reshape(-1, tile_rows, width) for part in arrived]
    count = picks.shape[0] // 2
    limits = jnp.repeat(jnp.array([3, blocks[0].shape[0] - 1], jnp.int32), count)
    packed, squares = pl.pallas_call(
        place_kernel,
        in_specs=[pl.BlockSpec(memory_space=pltpu.SMEM)]
        + [pl.BlockSpec(memory_space=pl.ANY)] * 4,
        out_shape=[
            jax.ShapeDtypeStruct((count, tile_rows, width), arrived[0].dtype),
            jax.ShapeDtypeStruct((count, tile_rows, 1), jnp.float32),
        ],
        scratch_shapes=[pltpu.SemaphoreType.DMA((count,))],
        cost_estimate=pl.CostEstimate(
            flops=0, bytes_accessed=4 * count * tile_rows * width, transcendentals=0
        ),
    )(jnp.clip(picks, 0, limits), *blocks)
    return packed.reshape(-1, width), squares.reshape(-1, 1)


def ring_body(
    activations,
    tile_dest,
    segment_ids,
    norm_gain,
    q_weight,
    k_weight,
    v_weight,
    q_bias,
    k_bias,
    v_bias,
    o_weight,
):
    z = lax.axis_index("dp")
    y = lax.axis_index("groups")
    x = lax.axis_index("tensor")
    core = lax.axis_index("pair")
    t = x * 2 + core
    slots, tile_rows = tile_dest.shape[1], segment_ids.shape[2]
    width = activations.shape[1]
    rows = TPD * tile_rows
    peers = 2
    q_share = q_weight.shape[1] // 2

    kv_at = (core * 2 + y) * HEAD
    q_own = lax.dynamic_slice_in_dim(q_weight, y * q_share, q_share, 1)
    k_own = lax.dynamic_slice_in_dim(k_weight, kv_at, HEAD, 1)
    v_own = lax.dynamic_slice_in_dim(v_weight, kv_at, HEAD, 1)
    qkv_own = jnp.concatenate([q_own, k_own, v_own], axis=1)
    o_own = lax.dynamic_slice_in_dim(o_weight, y * q_share, q_share, 0)
    bias = jnp.concatenate(
        [
            lax.dynamic_slice_in_dim(q_bias, y * q_share, q_share, 0),
            lax.dynamic_slice_in_dim(k_bias, kv_at, HEAD, 0),
            lax.dynamic_slice_in_dim(v_bias, kv_at, HEAD, 0),
        ]
    ).astype(jnp.float32)[None, :]

    def hop(up, down):
        s = len(up)
        up.append(shift(up[-1], "dp", [(i, i + 1) for i in range(s - 1, 3)]))
        down.append(shift(down[-1], "dp", [(i + 1, i) for i in range(0, 4 - s)]))

    q_up, q_down = [qkv_own], [qkv_own]
    hop(q_up, q_down)

    own_plan = lax.dynamic_index_in_dim(tile_dest, z, 0, keepdims=False)
    slot_ids = jnp.arange(slots, dtype=jnp.int32)
    peer_ids = jnp.arange(peers, dtype=jnp.int32)
    partners = jnp.arange(4, dtype=jnp.int32) ^ z
    same_before = (own_plan[None, :] == own_plan[:, None]) & (slot_ids[None, :] < slot_ids[:, None])
    send_rank = jnp.sum(same_before.astype(jnp.int32), axis=1)
    chooser = (own_plan[None, None, :] == partners[:, None, None]) & (
        send_rank[None, None, :] == peer_ids[None, :, None]
    )
    send_slots = jnp.sum(chooser.astype(jnp.int32) * slot_ids, axis=2).reshape(-1)
    outgoing = pack_tiles(send_slots, activations, tile_rows)
    arrived = [outgoing[0]] + [
        shift(outgoing[m], "dp", [(i, i ^ m) for i in range(4)]) for m in range(1, 4)
    ]
    *arrived, q_up[1], q_down[1], o_own = lax.optimization_barrier(
        (*arrived, q_up[1], q_down[1], o_own)
    )
    hop(q_up, q_down)
    o_up, o_down = [o_own], [o_own]
    hop(o_up, o_down)
    to_here = (tile_dest == z).astype(jnp.int32)
    from_each = jnp.sum(to_here, axis=1)
    first_place = jnp.cumsum(from_each) - from_each
    tile_ids = jnp.arange(TPD, dtype=jnp.int32)
    inside = (tile_ids[:, None] >= first_place[None, :]) & (
        tile_ids[:, None] < (first_place + from_each)[None, :]
    )
    source = jnp.sum(inside.astype(jnp.int32) * jnp.arange(4, dtype=jnp.int32)[None, :], axis=1)
    rank = jnp.sum(inside.astype(jnp.int32) * (tile_ids[:, None] - first_place[None, :]), axis=1)
    packed, squares = place_tiles(
        jnp.concatenate([source ^ z, rank]), arrived, tile_rows
    )
    flat_member = (tile_dest.reshape(-1) == z).astype(jnp.int32)
    flat_rank = jnp.cumsum(flat_member) - 1
    picker = flat_member[None, :] * (flat_rank[None, :] == tile_ids[:, None]).astype(jnp.int32)
    segment = jnp.sum(picker[:, :, None] * segment_ids.reshape(-1, tile_rows)[None, :, :], axis=1)
    positions = tile_positions(segment).reshape(rows, 1)
    positions = jnp.concatenate([positions, shift(positions, "groups", SWAP)], axis=0)
    half = HEAD // 2
    inverse = jnp.power(
        jnp.float32(1000000.0), -2.0 * jnp.arange(half, dtype=jnp.float32) / HEAD
    )
    angles = positions.astype(jnp.float32) * inverse[None, :]
    cosine, sine = jnp.cos(angles), jnp.sin(angles)
    cosine = jnp.concatenate([cosine, cosine], axis=1)
    sine = jnp.concatenate([-sine, sine], axis=1)

    widened = packed.astype(jnp.float32)
    squares = squares + shift(squares, "pair", SWAP)
    squares = squares + shift(squares, "tensor", SWAP)
    gain = lax.dynamic_slice_in_dim(norm_gain, t * width, width, 0).astype(jnp.float32)
    normed = (widened * lax.rsqrt(squares / (4 * width) + norm_eps) * gain).astype(jnp.bfloat16)
    peer = shift(normed, "groups", SWAP)
    across_own = shift(normed, "tensor", SWAP)
    q_up[2], q_down[2], o_up[1], o_down[1], peer, across_own = lax.optimization_barrier(
        (q_up[2], q_down[2], o_up[1], o_down[1], peer, across_own)
    )
    hop(q_up, q_down)
    hop(o_up, o_down)
    here = jnp.concatenate([normed, peer], axis=0)
    across_peer = shift(peer, "tensor", SWAP)
    across_peer, q_up[3], q_down[3], o_up[2], o_down[2] = lax.optimization_barrier(
        (across_peer, q_up[3], q_down[3], o_up[2], o_down[2])
    )
    hop(o_up, o_down)
    across = jnp.concatenate([across_own, across_peer], axis=0)
    shares = [here, shift(here, "pair", SWAP), across, shift(across, "pair", SWAP)]

    def by_partner(up, down):
        first = jnp.where(z % 2 == 0, down[1], up[1])
        second = up[2] + down[2]
        third = jnp.where(z == 1, down[1], jnp.where(z == 2, up[1], up[3] + down[3]))
        return [up[0], first, second, third]

    q_blocks = by_partner(q_up[:3] + [q_up[2]], q_down[:3] + [q_down[2]])
    at = jnp.arange(4, dtype=jnp.int32) ^ z ^ t
    lin = linear_rows(at[:3], shares, q_blocks[:3])
    context = attend_rows(
        shares, at[3], by_partner(q_up, q_down)[3], lin, bias, cosine, sine, positions, tile_rows
    )
    context, o_up[3], o_down[3] = lax.optimization_barrier((context, o_up[3], o_down[3]))

    every = ("groups", "dp", "tensor", "pair")
    index = lambda zz, yy, xx, cc: ((yy * 4 + zz) * 2 + xx) * 2 + cc

    def project(block):
        return jnp.dot(context, block, preferred_element_type=jnp.float32)

    def to_chip(part, m, cores):
        pairs = []
        for zz in range(4):
            xd = (zz ^ m) // 2
            for cc in cores(zz):
                pairs += [(index(zz, i, 1 - xd, cc), index(zz, i, xd, cc)) for i in range(2)]
        return part + shift(part.astype(jnp.bfloat16), every, pairs).astype(jnp.float32)

    both = lambda zz: (0, 1)
    keeps_first = (z ^ core) % 2 == 0

    def halves(block):
        return jnp.split(block, 2, axis=1)

    def to_core(one, two):
        kept = project(jnp.where(keeps_first, one, two))
        sent = project(jnp.where(keeps_first, two, one)).astype(jnp.bfloat16)
        return kept + shift(sent, "pair", SWAP).astype(jnp.float32)

    def to_group(part):
        return part[:rows] + shift(part[rows:].astype(jnp.bfloat16), "groups", SWAP).astype(
            jnp.float32
        )

    o_first = jnp.where(z % 2 == 0, o_down[1], o_up[1])
    first = to_core(o_own, o_first)
    first = to_group(first)
    first = to_chip(first, 0, both)
    o_blocks = by_partner(o_up, o_down)
    second = [
        to_group(to_core(one, two)) for one, two in zip(halves(o_blocks[2]), halves(o_blocks[3]))
    ]
    first, second[1] = lax.optimization_barrier((first, second[1]))
    second = jnp.concatenate([to_chip(part, 2, both) for part in second], axis=1)
    total = jnp.where(z // 2 == x, first, second)
    return (packed.astype(jnp.float32) + total).astype(jnp.bfloat16)


def solution(mesh):
    shape = dict(mesh.shape)
    ringed = shape == {"groups": 2, "dp": 4, "tensor": 2, "pair": 2}
    return jax.shard_map(
        ring_body if ringed else body,
        mesh=mesh,
        in_specs=(
            P(("groups", "dp"), ("tensor", "pair")),
            P("groups", None),
            P("groups", None, None),
            P(),
            P("dp", ("tensor", "pair")),
            P("dp", "tensor"),
            P("dp", "tensor"),
            P(("tensor", "pair")),
            P("tensor"),
            P("tensor"),
            P(("tensor", "pair"), "dp"),
        ),
        out_specs=P(("groups", "dp"), ("tensor", "pair")),
        check_vma=False,
    )
```

```python
import math

import jax
import jax.numpy as jnp
from jax import lax
from jax.experimental import pallas as pl
from jax.experimental.pallas import tpu as pltpu
from jax.sharding import PartitionSpec as P

QHEADS = 32
KVH = 8
HEAD = 128
TPD = 4
GROUP_SIZE = QHEADS // KVH


norm_eps = 1e-06

def normalize(values, gain_vector):
    widened = values.astype(jnp.float32)
    meansq = jnp.mean(widened * widened, axis=-1, keepdims=True)
    return (widened * lax.rsqrt(meansq + norm_eps) * gain_vector.astype(jnp.float32)).astype(
        jnp.bfloat16
    )


def rotary(values, positions):
    half_size = values.shape[-1] // 2
    inverse = jnp.power(
        jnp.float32(1000000.0), -2.0 * jnp.arange(half_size, dtype=jnp.float32) / values.shape[-1]
    )
    angles = positions.astype(jnp.float32)[:, None] * inverse[None, :]
    cosine = jnp.cos(angles)[:, None, :]
    sine_part = jnp.sin(angles)[:, None, :]
    front_half = values[..., :half_size]
    back_half = values[..., half_size:]
    return jnp.concatenate(
        [front_half * cosine - back_half * sine_part, back_half * cosine + front_half * sine_part],
        axis=-1,
    )


def tile_positions(segment):
    earlier = (segment[..., None, :] < segment[..., :, None]).astype(jnp.int32)
    first_row = jnp.sum(earlier, axis=-1)
    return jnp.arange(segment.shape[-1], dtype=jnp.int32) - first_row


def attend_tiles(query_groups, key_rows, value_rows, segment):
    tile_rows = query_groups.shape[1]
    scores = jnp.einsum(
        "tqgsd,tkgd->tgsqk", query_groups, key_rows, preferred_element_type=jnp.float32
    )
    scores = scores * (1.0 / math.sqrt(query_groups.shape[-1]))
    places = jnp.arange(tile_rows, dtype=jnp.int32)
    allowed = (segment[:, :, None] == segment[:, None, :]) & (
        places[None, None, :] <= places[None, :, None]
    )
    scores = jnp.where(allowed[:, None, None, :, :], scores, -1e30)
    attn_probs = jax.nn.softmax(scores, axis=-1).astype(jnp.bfloat16)
    context = jnp.einsum(
        "tgsqk,tkgd->tqgsd", attn_probs, value_rows, preferred_element_type=jnp.float32
    )
    return context.astype(jnp.bfloat16)


def body(
    activations,
    tile_dest,
    segment_ids,
    norm_gain,
    q_weight,
    k_weight,
    v_weight,
    q_bias,
    k_bias,
    v_bias,
    o_weight,
):
    dp_count = lax.axis_size("dp")
    own_index = lax.axis_index("dp")
    pair_size = lax.axis_size("pair")
    pair_index = lax.axis_index("pair")
    slot_count = tile_dest.shape[1]
    tile_rows = segment_ids.shape[2]
    feature_share = activations.shape[1]
    peer_slots = (slot_count + dp_count - 1) // dp_count
    own_plan = lax.dynamic_index_in_dim(tile_dest, own_index, 0, keepdims=False)
    slot_ids = jnp.arange(slot_count, dtype=jnp.int32)
    targets = jnp.arange(dp_count, dtype=jnp.int32)
    peer_ids = jnp.arange(peer_slots, dtype=jnp.int32)
    earlier_same = (own_plan[None, :] == own_plan[:, None]) & (
        slot_ids[None, :] < slot_ids[:, None]
    )
    send_rank = jnp.sum(earlier_same.astype(jnp.int32), axis=1)
    chooser = (own_plan[None, None, :] == targets[:, None, None]) & (
        send_rank[None, None, :] == peer_ids[None, :, None]
    )
    own_tiles = activations.reshape(slot_count, tile_rows, feature_share)
    outgoing = jnp.einsum(
        "jps,srf->jprf", chooser.astype(jnp.bfloat16), own_tiles, preferred_element_type=jnp.float32
    ).astype(jnp.bfloat16)
    arrived = lax.all_to_all(outgoing, "dp", split_axis=0, concat_axis=0, tiled=True)
    to_here = (tile_dest == own_index).astype(jnp.int32)
    from_each = jnp.sum(to_here, axis=1)
    first_place = jnp.cumsum(from_each) - from_each
    place_of = first_place[:, None] + peer_ids[None, :]
    landed = peer_ids[None, :] < from_each[:, None]
    tile_ids = jnp.arange(TPD, dtype=jnp.int32)
    placer = (place_of[None, :, :] == tile_ids[:, None, None]) & landed[None, :, :]
    packed_tiles = jnp.einsum(
        "ksp,sprf->krf", placer.astype(jnp.bfloat16), arrived, preferred_element_type=jnp.float32
    ).astype(jnp.bfloat16)
    row_count = TPD * tile_rows
    packed = packed_tiles.reshape(row_count, feature_share)
    flat_plan = tile_dest.reshape(-1)
    flat_member = (flat_plan == own_index).astype(jnp.int32)
    flat_rank = jnp.cumsum(flat_member) - 1
    picker = flat_member[None, :] * (flat_rank[None, :] == tile_ids[:, None]).astype(jnp.int32)
    flat_segments = segment_ids.reshape(-1, tile_rows)
    segment = jnp.sum(picker[:, :, None] * flat_segments[None, :, :], axis=1)
    positions = tile_positions(segment).reshape(row_count)
    whole_rows = lax.all_gather(packed, ("tensor", "pair"), axis=1, tiled=True)
    normed = normalize(whole_rows, norm_gain)
    q_width = q_weight.shape[1]
    kv_width = k_weight.shape[1]
    q_lin = jnp.dot(
        normed,
        lax.all_gather(q_weight, "dp", axis=0, tiled=True),
        preferred_element_type=jnp.float32,
    )
    k_lin = jnp.dot(
        normed,
        lax.all_gather(k_weight, "dp", axis=0, tiled=True),
        preferred_element_type=jnp.float32,
    )
    v_lin = jnp.dot(
        normed,
        lax.all_gather(v_weight, "dp", axis=0, tiled=True),
        preferred_element_type=jnp.float32,
    )
    q_heads = q_width // HEAD
    kv_heads = kv_width // HEAD
    queries = rotary(
        (q_lin + q_bias.astype(jnp.float32)).reshape(row_count, q_heads, HEAD), positions
    ).astype(jnp.bfloat16)
    keys_local = rotary(
        (k_lin + k_bias.astype(jnp.float32)).reshape(-1, kv_heads, HEAD), positions
    ).astype(jnp.bfloat16)
    values_local = (
        (v_lin + v_bias.astype(jnp.float32)).astype(jnp.bfloat16).reshape(-1, kv_heads, HEAD)
    )
    key_rows, value_rows = (keys_local, values_local)
    group_size = QHEADS // KVH
    kv_count = max(1, q_heads // group_size)
    group_span = q_heads // kv_count
    kv_first = pair_index * q_heads // group_size
    key_rows = lax.dynamic_slice_in_dim(key_rows, kv_first, kv_count, 1).reshape(
        TPD, tile_rows, kv_count, HEAD
    )
    value_rows = lax.dynamic_slice_in_dim(value_rows, kv_first, kv_count, 1).reshape(
        TPD, tile_rows, kv_count, HEAD
    )
    query_groups = queries.reshape(TPD, tile_rows, kv_count, group_span, HEAD)
    context = attend_tiles(query_groups, key_rows, value_rows, segment).reshape(
        row_count, q_heads * HEAD
    )
    partials = jnp.dot(
        context,
        lax.all_gather(o_weight, "dp", axis=1, tiled=True),
        preferred_element_type=jnp.float32,
    )
    full_sums = lax.psum(partials.astype(jnp.bfloat16), ("tensor", "pair")).astype(jnp.float32)
    my_slot = lax.axis_index("tensor") * pair_size + pair_index
    summed = lax.dynamic_slice_in_dim(full_sums, my_slot * feature_share, feature_share, 1)
    return (packed.astype(jnp.float32) + summed).astype(jnp.bfloat16)


def shift(values, axis, pairs):
    return lax.ppermute(values, axis, pairs)


SWAP = [(0, 1), (1, 0)]


def fetch_share(which, shares, target, sem):
    def each(act):
        for k, share in enumerate(shares):

            @pl.when(which == k)
            def _():
                act(pltpu.make_async_copy(share, target, sem))

    return each


def linear_kernel(at_ref, *refs):
    shares, blocks = refs[:4], refs[4:7]
    out_ref, share_buf, block_buf, sems = refs[7:]
    fetches = []
    for m in range(3):
        fetches.append(fetch_share(at_ref[m], shares, share_buf.at[m], sems.at[m]))
        fetches[m](lambda copy: copy.start())
        pltpu.make_async_copy(blocks[m], block_buf.at[m], sems.at[3 + m]).start()
    for m in range(3):
        fetches[m](lambda copy: copy.wait())
        pltpu.make_async_copy(blocks[m], block_buf.at[m], sems.at[3 + m]).wait()
    step = 128

    @pl.loop(0, out_ref.shape[0] // step)
    def _(i):
        at = pl.ds(pl.multiple_of(i * step, step), step)
        total = None
        for m in range(3):
            part = jnp.dot(share_buf[m, at], block_buf[m], preferred_element_type=jnp.float32)
            total = part if total is None else total + part
        out_ref[at] = total


def linear_rows(at, shares, blocks):
    (count, depth), width = shares[0].shape, blocks[0].shape[1]
    return pl.pallas_call(
        linear_kernel,
        in_specs=[pl.BlockSpec(memory_space=pltpu.SMEM)]
        + [pl.BlockSpec(memory_space=pl.ANY)] * 7,
        out_specs=pl.BlockSpec(memory_space=pltpu.VMEM),
        out_shape=jax.ShapeDtypeStruct((count, width), jnp.float32),
        scratch_shapes=[
            pltpu.VMEM((3, count, depth), jnp.bfloat16),
            pltpu.VMEM((3, depth, width), jnp.bfloat16),
            pltpu.SemaphoreType.DMA((6,)),
        ],
        compiler_params=pltpu.CompilerParams(vmem_limit_bytes=32 * 1024 * 1024),
    )(at, *shares, *blocks)


def attention_kernel(at_ref, *refs):
    shares, refs = refs[:4], refs[4:]
    block_ref, lin_ref, bias_ref, cos_ref, sin_ref, pos_ref, out_ref, share_buf, sem = refs
    step = pl.program_id(0)

    @pl.when(step == 0)
    def _():
        fetch = fetch_share(at_ref[0], shares, share_buf, sem)
        fetch(lambda copy: copy.start())
        fetch(lambda copy: copy.wait())

    own = pl.ds(pl.multiple_of(step * lin_ref.shape[0], lin_ref.shape[0]), lin_ref.shape[0])

    heads = out_ref.shape[1] // HEAD
    rows = lin_ref.shape[0]
    lin = lin_ref[...] + jnp.dot(
        share_buf[own], block_ref[...], preferred_element_type=jnp.float32
    )
    lin = lin + bias_ref[...]
    cosine = cos_ref[...]
    sine = sin_ref[...]

    def rotate(values):
        return (values * cosine + pltpu.roll(values, HEAD // 2, 1) * sine).astype(jnp.bfloat16)

    queries = jnp.concatenate(
        [rotate(lin[:, h * HEAD : (h + 1) * HEAD]) for h in range(heads)], axis=0
    )
    keys = rotate(lin[:, heads * HEAD : (heads + 1) * HEAD])
    value_rows = lin[:, (heads + 1) * HEAD :].astype(jnp.bfloat16)
    scores = lax.dot_general(
        queries, keys, (((1,), (1,)), ((), ())), preferred_element_type=jnp.float32
    )
    scores = (scores * (1.0 / math.sqrt(HEAD))).reshape(heads, rows, rows)
    row = lax.broadcasted_iota(jnp.int32, (rows, rows), 0)
    column = lax.broadcasted_iota(jnp.int32, (rows, rows), 1)
    allowed = (column <= row) & (column >= row - pos_ref[...])
    scores = jnp.where(allowed[None], scores, -1e30)
    largest = jnp.max(scores, axis=-1, keepdims=True)
    weights = jnp.exp(scores - largest)
    probs = (weights / jnp.sum(weights, axis=-1, keepdims=True)).astype(jnp.bfloat16)
    context = lax.dot_general(
        probs.reshape(heads * rows, rows),
        value_rows,
        (((1,), (0,)), ((), ())),
        preferred_element_type=jnp.float32,
    ).astype(jnp.bfloat16)
    for h in range(heads):
        out_ref[:, h * HEAD : (h + 1) * HEAD] = context[h * rows : (h + 1) * rows]


def attend_rows(shares, at, block, lin, bias, cosine, sine, positions, tile_rows):
    count, width = lin.shape
    out_width = width - 2 * HEAD
    by_tile = lambda w: pl.BlockSpec((tile_rows, w), lambda i, at: (i, 0))
    return pl.pallas_call(
        attention_kernel,
        grid_spec=pltpu.PrefetchScalarGridSpec(
            num_scalar_prefetch=1,
            grid=(count // tile_rows,),
            in_specs=[
                *[pl.BlockSpec(memory_space=pl.ANY)] * 4,
                pl.BlockSpec(block.shape, lambda i, at: (0, 0)),
                by_tile(width),
                pl.BlockSpec((1, width), lambda i, at: (0, 0)),
                by_tile(HEAD),
                by_tile(HEAD),
                by_tile(1),
            ],
            out_specs=by_tile(out_width),
            scratch_shapes=[
                pltpu.VMEM(shares[0].shape, jnp.bfloat16),
                pltpu.SemaphoreType.DMA(()),
            ],
        ),
        out_shape=jax.ShapeDtypeStruct((count, out_width), jnp.bfloat16),
        compiler_params=pltpu.CompilerParams(vmem_limit_bytes=32 * 1024 * 1024),
    )(at.reshape(1), *shares, block, lin, bias, cosine, sine, positions)


def pack_kernel(slots_ref, *refs):
    for m in range(4):
        refs[4 + m][...] = refs[m][...]


def pack_tiles(send_slots, activations, tile_rows):
    width = activations.shape[1]
    tiles = activations.reshape(-1, tile_rows, width)
    peers = send_slots.shape[0] // 4
    block = (1, tile_rows, width)
    pick = lambda m: pl.BlockSpec(block, lambda p, slots: (slots[m * peers + p], 0, 0))
    outs = pl.pallas_call(
        pack_kernel,
        grid_spec=pltpu.PrefetchScalarGridSpec(
            num_scalar_prefetch=1,
            grid=(peers,),
            in_specs=[pick(m) for m in range(4)],
            out_specs=[pl.BlockSpec(block, lambda p, slots: (p, 0, 0))] * 4,
        ),
        out_shape=[jax.ShapeDtypeStruct((peers, tile_rows, width), activations.dtype)] * 4,
        cost_estimate=pl.CostEstimate(
            flops=0, bytes_accessed=4 * activations.size, transcendentals=0
        ),
    )(jnp.clip(send_slots, 0, tiles.shape[0] - 1), *[tiles] * 4)
    return [out.reshape(peers * tile_rows, width) for out in outs]


def place_kernel(picks_ref, *refs):
    arrived, (packed_ref, squares_ref, sems) = refs[:4], refs[4:]
    count = packed_ref.shape[0]

    def each(act):
        for k in range(count):
            for m in range(4):

                @pl.when(picks_ref[k] == m)
                def _():
                    act(
                        pltpu.make_async_copy(
                            arrived[m].at[picks_ref[count + k]], packed_ref.at[k], sems.at[k]
                        )
                    )

    each(lambda copy: copy.start())
    each(lambda copy: copy.wait())
    for k in range(count):
        widened = packed_ref[k].astype(jnp.float32)
        squares_ref[k] = jnp.sum(widened * widened, axis=-1, keepdims=True)


def place_tiles(picks, arrived, tile_rows):
    width = arrived[0].shape[1]
    blocks = [part.reshape(-1, tile_rows, width) for part in arrived]
    count = picks.shape[0] // 2
    limits = jnp.repeat(jnp.array([3, blocks[0].shape[0] - 1], jnp.int32), count)
    packed, squares = pl.pallas_call(
        place_kernel,
        in_specs=[pl.BlockSpec(memory_space=pltpu.SMEM)]
        + [pl.BlockSpec(memory_space=pl.ANY)] * 4,
        out_shape=[
            jax.ShapeDtypeStruct((count, tile_rows, width), arrived[0].dtype),
            jax.ShapeDtypeStruct((count, tile_rows, 1), jnp.float32),
        ],
        scratch_shapes=[pltpu.SemaphoreType.DMA((count,))],
        cost_estimate=pl.CostEstimate(
            flops=0, bytes_accessed=4 * count * tile_rows * width, transcendentals=0
        ),
    )(jnp.clip(picks, 0, limits), *blocks)
    return packed.reshape(-1, width), squares.reshape(-1, 1)


def ring_body(
    activations,
    tile_dest,
    segment_ids,
    norm_gain,
    q_weight,
    k_weight,
    v_weight,
    q_bias,
    k_bias,
    v_bias,
    o_weight,
):
    z = lax.axis_index("dp")
    y = lax.axis_index("groups")
    x = lax.axis_index("tensor")
    core = lax.axis_index("pair")
    t = x * 2 + core
    slots, tile_rows = tile_dest.shape[1], segment_ids.shape[2]
    width = activations.shape[1]
    rows = TPD * tile_rows
    peers = 2
    q_share = q_weight.shape[1] // 2

    kv_at = (core * 2 + y) * HEAD
    q_own = lax.dynamic_slice_in_dim(q_weight, y * q_share, q_share, 1)
    k_own = lax.dynamic_slice_in_dim(k_weight, kv_at, HEAD, 1)
    v_own = lax.dynamic_slice_in_dim(v_weight, kv_at, HEAD, 1)
    qkv_own = jnp.concatenate([q_own, k_own, v_own], axis=1)
    o_own = lax.dynamic_slice_in_dim(o_weight, y * q_share, q_share, 0)
    bias = jnp.concatenate(
        [
            lax.dynamic_slice_in_dim(q_bias, y * q_share, q_share, 0),
            lax.dynamic_slice_in_dim(k_bias, kv_at, HEAD, 0),
            lax.dynamic_slice_in_dim(v_bias, kv_at, HEAD, 0),
        ]
    ).astype(jnp.float32)[None, :]

    def hop(up, down):
        s = len(up)
        up.append(shift(up[-1], "dp", [(i, i + 1) for i in range(s - 1, 3)]))
        down.append(shift(down[-1], "dp", [(i + 1, i) for i in range(0, 4 - s)]))

    q_up, q_down = [qkv_own], [qkv_own]
    hop(q_up, q_down)

    own_plan = lax.dynamic_index_in_dim(tile_dest, z, 0, keepdims=False)
    slot_ids = jnp.arange(slots, dtype=jnp.int32)
    peer_ids = jnp.arange(peers, dtype=jnp.int32)
    partners = jnp.arange(4, dtype=jnp.int32) ^ z
    same_before = (own_plan[None, :] == own_plan[:, None]) & (slot_ids[None, :] < slot_ids[:, None])
    send_rank = jnp.sum(same_before.astype(jnp.int32), axis=1)
    chooser = (own_plan[None, None, :] == partners[:, None, None]) & (
        send_rank[None, None, :] == peer_ids[None, :, None]
    )
    send_slots = jnp.sum(chooser.astype(jnp.int32) * slot_ids, axis=2).reshape(-1)
    outgoing = pack_tiles(send_slots, activations, tile_rows)
    arrived = [outgoing[0]] + [
        shift(outgoing[m], "dp", [(i, i ^ m) for i in range(4)]) for m in range(1, 4)
    ]
    *arrived, q_up[1], q_down[1] = lax.optimization_barrier((*arrived, q_up[1], q_down[1]))
    hop(q_up, q_down)
    to_here = (tile_dest == z).astype(jnp.int32)
    from_each = jnp.sum(to_here, axis=1)
    first_place = jnp.cumsum(from_each) - from_each
    tile_ids = jnp.arange(TPD, dtype=jnp.int32)
    inside = (tile_ids[:, None] >= first_place[None, :]) & (
        tile_ids[:, None] < (first_place + from_each)[None, :]
    )
    source = jnp.sum(inside.astype(jnp.int32) * jnp.arange(4, dtype=jnp.int32)[None, :], axis=1)
    rank = jnp.sum(inside.astype(jnp.int32) * (tile_ids[:, None] - first_place[None, :]), axis=1)
    packed, squares = place_tiles(
        jnp.concatenate([source ^ z, rank]), arrived, tile_rows
    )
    flat_member = (tile_dest.reshape(-1) == z).astype(jnp.int32)
    flat_rank = jnp.cumsum(flat_member) - 1
    picker = flat_member[None, :] * (flat_rank[None, :] == tile_ids[:, None]).astype(jnp.int32)
    segment = jnp.sum(picker[:, :, None] * segment_ids.reshape(-1, tile_rows)[None, :, :], axis=1)
    positions = tile_positions(segment).reshape(rows, 1)
    positions = jnp.concatenate([positions, shift(positions, "groups", SWAP)], axis=0)
    half = HEAD // 2
    inverse = jnp.power(
        jnp.float32(1000000.0), -2.0 * jnp.arange(half, dtype=jnp.float32) / HEAD
    )
    angles = positions.astype(jnp.float32) * inverse[None, :]
    cosine, sine = jnp.cos(angles), jnp.sin(angles)
    cosine = jnp.concatenate([cosine, cosine], axis=1)
    sine = jnp.concatenate([-sine, sine], axis=1)

    widened = packed.astype(jnp.float32)
    squares = squares + shift(squares, "pair", SWAP)
    squares = squares + shift(squares, "tensor", SWAP)
    gain = lax.dynamic_slice_in_dim(norm_gain, t * width, width, 0).astype(jnp.float32)
    normed = (widened * lax.rsqrt(squares / (4 * width) + norm_eps) * gain).astype(jnp.bfloat16)
    peer = shift(normed, "groups", SWAP)
    across_own = shift(normed, "tensor", SWAP)
    q_up[2], q_down[2], peer, across_own, o_own = lax.optimization_barrier(
        (q_up[2], q_down[2], peer, across_own, o_own)
    )
    hop(q_up, q_down)
    o_up, o_down = [o_own], [o_own]
    hop(o_up, o_down)
    here = jnp.concatenate([normed, peer], axis=0)
    across_peer = shift(peer, "tensor", SWAP)
    across_peer, q_up[3], q_down[3], o_up[1], o_down[1] = lax.optimization_barrier(
        (across_peer, q_up[3], q_down[3], o_up[1], o_down[1])
    )
    hop(o_up, o_down)
    across = jnp.concatenate([across_own, across_peer], axis=0)
    shares = [here, shift(here, "pair", SWAP), across, shift(across, "pair", SWAP)]

    def by_partner(up, down):
        first = jnp.where(z % 2 == 0, down[1], up[1])
        second = up[2] + down[2]
        third = jnp.where(z == 1, down[1], jnp.where(z == 2, up[1], up[3] + down[3]))
        return [up[0], first, second, third]

    q_blocks = by_partner(q_up[:3] + [q_up[2]], q_down[:3] + [q_down[2]])
    at = jnp.arange(4, dtype=jnp.int32) ^ z ^ t
    lin = linear_rows(at[:3], shares, q_blocks[:3])
    context = attend_rows(
        shares, at[3], by_partner(q_up, q_down)[3], lin, bias, cosine, sine, positions, tile_rows
    )
    context, o_up[2], o_down[2] = lax.optimization_barrier((context, o_up[2], o_down[2]))
    hop(o_up, o_down)

    every = ("groups", "dp", "tensor", "pair")
    index = lambda zz, yy, xx, cc: ((yy * 4 + zz) * 2 + xx) * 2 + cc

    def project(block):
        return jnp.dot(context, block, preferred_element_type=jnp.float32)

    def to_chip(part, m, cores):
        pairs = []
        for zz in range(4):
            xd = (zz ^ m) // 2
            for cc in cores(zz):
                pairs += [(index(zz, i, 1 - xd, cc), index(zz, i, xd, cc)) for i in range(2)]
        return part + shift(part.astype(jnp.bfloat16), every, pairs).astype(jnp.float32)

    both = lambda zz: (0, 1)
    keeps_first = (z ^ core) % 2 == 0

    def halves(block):
        return jnp.split(block, 2, axis=1)

    def to_core(one, two):
        kept = project(jnp.where(keeps_first, one, two))
        sent = project(jnp.where(keeps_first, two, one)).astype(jnp.bfloat16)
        return kept + shift(sent, "pair", SWAP).astype(jnp.float32)

    def to_group(part):
        return part[:rows] + shift(part[rows:].astype(jnp.bfloat16), "groups", SWAP).astype(
            jnp.float32
        )

    o_first = jnp.where(z % 2 == 0, o_down[1], o_up[1])
    first = to_core(o_own, o_first)
    first = to_group(first)
    first, o_up[3], o_down[3] = lax.optimization_barrier((first, o_up[3], o_down[3]))
    first = to_chip(first, 0, both)
    o_blocks = by_partner(o_up, o_down)
    second = [
        to_group(to_core(one, two)) for one, two in zip(halves(o_blocks[2]), halves(o_blocks[3]))
    ]
    first, second[1] = lax.optimization_barrier((first, second[1]))
    second = jnp.concatenate([to_chip(part, 2, both) for part in second], axis=1)
    total = jnp.where(z // 2 == x, first, second)
    return (packed.astype(jnp.float32) + total).astype(jnp.bfloat16)


def solution(mesh):
    shape = dict(mesh.shape)
    ringed = shape == {"groups": 2, "dp": 4, "tensor": 2, "pair": 2}
    return jax.shard_map(
        ring_body if ringed else body,
        mesh=mesh,
        in_specs=(
            P(("groups", "dp"), ("tensor", "pair")),
            P("groups", None),
            P("groups", None, None),
            P(),
            P("dp", ("tensor", "pair")),
            P("dp", "tensor"),
            P("dp", "tensor"),
            P(("tensor", "pair")),
            P("tensor"),
            P("tensor"),
            P(("tensor", "pair"), "dp"),
        ),
        out_specs=P(("groups", "dp"), ("tensor", "pair")),
        check_vma=False,
    )
```
